32 devices in a mesh: fsdp: 8 (over y, x, core), tensor: 4 (over z).
Axes of the slice: x: 2, y: 2, z: 4, core: 2. Of those that a mesh axis runs over, the one named last changes fastest.
Arguments:
- tokens: bfloat16 [1024, 8192], P('tensor', 'fsdp'), may hold values from -6 to 6
- gate_weight: bfloat16 [8192, 14336], P('fsdp', 'tensor'), may hold values from -0.0625 to 0.0625
- up_weight: bfloat16 [8192, 14336], P('fsdp', 'tensor'), may hold values from -0.0625 to 0.0625
- down_frozen: bfloat16 [14336, 8192], P('tensor', 'fsdp'), may hold values from -0.046875 to 0.046875
- down_learn: bfloat16 [14336, 8192], P('tensor', 'fsdp'), may hold values from -0.046875 to 0.046875
- steer: float32 [8192], replicated, may hold values from -6 to 6
- sample_lengths: int32 [2, 4], replicated, may hold values from 1 to 128, 320 in all within a row
Outputs:
- grad_down: float32 [14336, 8192], P('tensor', 'fsdp')
- losses: float32 [2], replicated
The draws below stay inside these ranges and needn't reach their ends.
Inputs may be any that keep to these rules, and one draw needn't show every extreme that they name: `sample_lengths`: in each row, the lengths sum to 320 and one sample has exactly 128 live tokens.
All inputs are finite; a program needn't handle non-finite values.
Results may differ from the reference program's by a relative error of at most 0.0047.
Values may be sent and summed in bfloat16 or wider, within the bound.
No kernel may reach another device: no remote copies, remote signals or barrier semaphores. Data moves between devices by JAX's collectives and lax.ppermute only.
A program may use at most 128 MiB of HBM per device.

```python
import math
import jax
import jax.numpy as jnp
import numpy as np

D = 8192
FF = 14336
SLOT = 128
SEQS = 4
TOKENS = 1024
LIVE = 320


def shard_levels(key, shape, split, smallest, largest):
    loudness = 1.0
    for position, parts in split:
        heights = jax.random.uniform(jax.random.fold_in(jax.random.fold_in(key, 6), position), (parts,), jnp.float32, smallest / len(split), largest / len(split))
        loudness = loudness * jnp.repeat(jnp.exp(heights), shape[position] // parts).reshape((-1,) + (1,) * (len(shape) - 1 - position))
    return loudness


def split_up(number_of, total, bound, skew):
    portions = [(1 << 20) // math.isqrt(rank ** skew) + 1 for rank in range(2, number_of + 1)]
    spare, counts = total - bound - (number_of - 1), [1] * (number_of - 1)
    while spare > 0:
        free = [i for i in range(number_of - 1) if counts[i] < bound]
        whole, budget = sum([portions[i] for i in free]), spare
        for i in free:
            more = min(bound - counts[i], max(1, budget * portions[i] // whole), spare)
            counts[i] = counts[i] + more
            spare = spare - more
    return np.array([bound] + counts)


def uneven(stream_key, count, total, limit, slope):
    if count == 2:
        one = jax.random.randint(stream_key, (), max(1, total - limit), min(limit, total - 1) + 1)
        return jnp.stack([one, total - one])
    tallies = jnp.asarray(split_up(count, total, limit, slope), jnp.int32)
    twos = (count - 1) // 2
    source_of, taker = tallies[1:1 + 2 * twos:2], tallies[2:2 + 2 * twos:2]
    margin = jnp.minimum(source_of - 1, limit - taker)
    shifted = jax.random.randint(jax.random.fold_in(stream_key, 1), (twos,), 0, 1 << 20) % (margin + 1)
    tallies = tallies.at[1:1 + 2 * twos:2].set(source_of - shifted).at[2:2 + 2 * twos:2].set(taker + shifted)
    return tallies[jax.random.permutation(jax.random.fold_in(stream_key, 2), count)]


def scatter_about(own_key, shape, spread, reach, shards=(), kind=jnp.bfloat16):
    entries = spread * jax.random.normal(own_key, shape, jnp.float32)
    if shards:
        entries = entries * shard_levels(own_key, shape, shards, -0.22, 0.18)
    return jnp.clip(entries, -reach, reach).astype(kind)


def setup_inputs(seed: int = 0) -> dict:
    key_of = jax.random.split(jax.random.key(seed), 8)
    tokens = scatter_about(key_of[0], (TOKENS, D), 1.0, 6.0, ((0, 4), (1, 8)))
    gate_weight = scatter_about(key_of[1], (D, FF), D ** -0.5, 0.0625, ((0, 8), (1, 4)))
    up_weight = scatter_about(key_of[2], (D, FF), D ** -0.5, 0.0625, ((0, 8), (1, 4)))
    down_frozen = scatter_about(key_of[3], (FF, D), FF ** -0.5, 0.046875, ((0, 4), (1, 8)))
    down_learn = scatter_about(key_of[4], (FF, D), FF ** -0.5, 0.046875, ((0, 4), (1, 8)))
    steer = scatter_about(key_of[5], (D,), 1.0, 6.0, (), jnp.float32)
    sample_lengths = jax.vmap(lambda own: uneven(own, SEQS, LIVE, SLOT, 0))(jax.random.split(key_of[6], 2)).reshape((2, SEQS)).astype(jnp.int32)
    return {"tokens": tokens, "gate_weight": gate_weight, "up_weight": up_weight, "down_frozen": down_frozen, "down_learn": down_learn, "steer": steer, "sample_lengths": sample_lengths}


def reference(tokens, gate_weight, up_weight, down_frozen, down_learn, steer, sample_lengths):
    gate = jnp.dot(tokens, gate_weight, preferred_element_type=jnp.float32)
    up = jnp.dot(tokens, up_weight, preferred_element_type=jnp.float32)
    hidden = (jax.nn.silu(gate) * up).astype(jnp.bfloat16)
    base = tokens.astype(jnp.float32)
    out_frozen = base + jnp.dot(hidden, down_frozen, preferred_element_type=jnp.float32)
    out_learn = base + jnp.dot(hidden, down_learn, preferred_element_type=jnp.float32)
    row_ids = jnp.arange(TOKENS).astype(jnp.int32)
    flat = sample_lengths.reshape(-1)
    row_len = flat[(row_ids // SLOT).astype(jnp.int32)]
    live = row_ids % SLOT < row_len
    forget = (live & (row_ids < SEQS * SLOT))[:, None]
    retain = (live & (row_ids >= SEQS * SLOT))[:, None]
    steer32 = steer.astype(jnp.float32)
    target = 20.0 * steer32 / jnp.sqrt(D * (jnp.mean(steer32 * steer32) + 1e-06))
    steer_diff = out_learn - target[None, :]
    keep_diff = out_learn - out_frozen
    zero = jnp.zeros((), jnp.float32)
    sum_steer = jnp.sum(jnp.where(forget, steer_diff * steer_diff, zero))
    sum_keep = jnp.sum(jnp.where(retain, keep_diff * keep_diff, zero))
    count_f = jnp.sum(sample_lengths[0]).astype(jnp.float32)
    count_r = jnp.sum(sample_lengths[1]).astype(jnp.float32)
    losses = jnp.stack([sum_steer / (count_f * D), sum_keep / (count_r * D)])
    delta = (jnp.where(forget, steer_diff, zero) + 2.0 * jnp.where(retain, keep_diff, zero)).astype(jnp.bfloat16)
    grad_down = jax.lax.dot_general(hidden, delta, (((0,), (0,)), ((), ())), preferred_element_type=jnp.float32)
    return (grad_down, losses)
```

```python
import math

import jax
import jax.numpy as jnp
from jax import lax
from jax.sharding import PartitionSpec as P

D = 8192
SLOT = 128
TOKEN_BOUND = 6.0
WEIGHT_BOUND = 0.0625
HALF_MAX = 65504.0
B_PARTS = 2
f32 = jnp.float32
bf16 = jnp.bfloat16
f16 = jnp.float16


def slot_lengths(slot_ids, flat, sample_count):
    sample_ids = jnp.arange(sample_count, dtype=jnp.int32)
    return jnp.sum(jnp.where(slot_ids[:, None] == sample_ids[None, :], flat[None, :], 0), axis=1)


def dot(a, b):
    return jnp.dot(a, b, preferred_element_type=f32)


def swap(axis, n, bit, x):
    return lax.ppermute(x, axis, [(i, i ^ bit) for i in range(n)])


def by_core(axis_bits, x):
    even, odd = axis_bits
    return lax.ppermute(x, "fsdp", [(i, i ^ (odd if i % 2 else even)) for i in range(8)])


FIRST = (2, 4)
SECOND = (4, 2)


def swap_middle(x):
    q = x.shape[0] // 4
    return jnp.concatenate([x[:q], x[2 * q : 3 * q], x[q : 2 * q], x[3 * q :]], axis=0)


def paired_shards(tokens, gate_weight, up_weight, down_frozen, down_learn, steer, sample_lengths):
    cols = tokens.shape[1]
    slots = tokens.shape[0]
    width = gate_weight.shape[1]
    half = width // 2
    seqs = sample_lengths.shape[1]
    rows = seqs * SLOT * 5 // 8
    n_fsdp = lax.axis_size("fsdp")
    n_tensor = lax.axis_size("tensor")
    total = cols * n_fsdp
    scale = 2.0 ** math.floor(math.log2(HALF_MAX / (TOKEN_BOUND * WEIGHT_BOUND * total)))
    me_f = lax.axis_index("fsdp")
    me_t = lax.axis_index("tensor")
    core = me_f % 2
    chip = me_f // 2
    kind_a = me_t // 2
    first_is_forget = kind_a == 0

    other_tokens = swap("tensor", n_tensor, 1, tokens)

    def column_half(w, which):
        return lax.dynamic_slice_in_dim(w, which * half, half, 1)

    w_give = jnp.concatenate(
        [column_half(gate_weight, 1 - core), column_half(up_weight, 1 - core)], axis=1
    )
    w_sib = swap("fsdp", n_fsdp, 1, w_give)
    w_own = jnp.concatenate([column_half(gate_weight, core), column_half(up_weight, core)], axis=1)

    lengths = jnp.where(first_is_forget, sample_lengths[0], sample_lengths[1])
    before = jnp.cumsum(lengths) - lengths

    def pick(block_of_slots):
        slot_ids = block_of_slots * slots + jnp.arange(slots, dtype=jnp.int32)
        sample = slot_ids // SLOT
        inside = slot_ids % SLOT
        length = slot_lengths(sample, lengths, seqs)
        position = slot_lengths(sample, before, seqs) + inside
        position = jnp.where(inside < length, position, -1)
        row = jnp.arange(rows, dtype=jnp.int32)
        quarter = rows // 4
        b = row // quarter
        swapped = jnp.where(b == 1, 2, jnp.where(b == 2, 1, b))
        q = jnp.bitwise_xor(chip, jnp.where(core == 0, swapped, b))
        wanted = q * quarter + row % quarter
        return (wanted[:, None] == position[None, :]).astype(bf16)

    mine = me_t % 2
    x_a = dot(pick(mine), tokens) + dot(pick(1 - mine), other_tokens)
    x_a = x_a.astype(bf16)
    x_b = swap("tensor", n_tensor, 3, x_a)

    def hidden_of(x):
        x_sib = swap_middle(swap("fsdp", n_fsdp, 1, x))
        r = x.shape[0]

        def part(lo, hi):
            return (dot(x[lo:hi], w_own) + dot(x_sib[lo:hi], w_sib)) * scale

        give = part(r // 2, r).astype(f16)
        got = by_core(FIRST, give)
        keep = part(0, r // 2)
        give = (keep[r // 4 :] + got[r // 4 :].astype(f32)).astype(f16)
        keep = keep[: r // 4] + got[: r // 4].astype(f32)
        got = by_core(SECOND, give)
        summed = (keep + got.astype(f32)) * (1.0 / scale)
        own = (jax.nn.silu(summed[:, :half]) * summed[:, half:]).astype(bf16)
        own = jnp.concatenate([own, by_core(SECOND, own)], axis=0)
        own = jnp.concatenate([own, by_core(FIRST, own)], axis=0)
        sib = swap_middle(swap("fsdp", n_fsdp, 1, own))
        even = core == 0
        return jnp.concatenate([jnp.where(even, own, sib), jnp.where(even, sib, own)], axis=1)

    def down_of(hidden, is_forget):
        learn = dot(hidden, down_learn)
        frozen = dot(hidden, down_frozen)
        return learn - jnp.where(is_forget, 0.0, 1.0) * frozen

    def split(x):
        parts = x.reshape(4, B_PARTS, rows // 4 // B_PARTS, x.shape[1])
        return [parts[:, j].reshape(rows // B_PARTS, x.shape[1]) for j in range(B_PARTS)]

    def join(parts):
        r = rows // 4 // B_PARTS
        stacked = jnp.stack([p.reshape(4, r, p.shape[1]) for p in parts], axis=1)
        return stacked.reshape(rows, parts[0].shape[1])

    hidden_a = hidden_of(x_a)
    part_a = down_of(hidden_a, first_is_forget).astype(bf16)
    pair_a = part_a.astype(f32) + swap("tensor", n_tensor, 1, part_a).astype(f32)
    far = swap("tensor", n_tensor, 3, pair_a.astype(bf16))

    mean_square = jnp.mean(steer * steer)
    target_scale = 20.0 / jnp.sqrt(total * (mean_square + 1e-06))
    target = target_scale * lax.dynamic_slice_in_dim(steer, me_f * cols, cols)

    deltas_b = []
    deltas_a = []
    hiddens_b = []
    local = jnp.zeros((), f32)
    for x, far_part in zip(split(x_b), split(far)):
        hidden_b = hidden_of(x)
        part_b = down_of(hidden_b, ~first_is_forget).astype(bf16)
        total_b = (part_b.astype(f32) + swap("tensor", n_tensor, 1, part_b).astype(f32)) + far_part.astype(f32)
        diff = jnp.where(first_is_forget, total_b, total_b + x.astype(f32) - target[None, :])
        local = local + jnp.sum(diff * diff)
        delta = (diff * jnp.where(first_is_forget, 2.0, 1.0)).astype(bf16)
        deltas_b.append(delta)
        deltas_a.append(swap("tensor", n_tensor, 3, delta))
        hiddens_b.append(hidden_b)

    value = jnp.full((8, 128), local, f32)
    for bit in (1, 2, 4):
        value = value + swap("fsdp", n_fsdp, bit, value)
    other = swap("tensor", n_tensor, 3, value)
    sum_steer = jnp.where(first_is_forget, other, value)[0, 0]
    sum_keep = jnp.where(first_is_forget, value, other)[0, 0]
    count_f = jnp.sum(sample_lengths[0]).astype(f32)
    count_r = jnp.sum(sample_lengths[1]).astype(f32)
    losses = jnp.stack([sum_steer / (count_f * total), sum_keep / (count_r * total)])

    hidden = jnp.concatenate([hidden_a] + hiddens_b, axis=0)
    delta = jnp.concatenate([join(deltas_a)] + deltas_b, axis=0)
    grad_down = lax.dot_general(
        hidden, delta, (((0,), (0,)), ((), ())), preferred_element_type=f32
    )
    return grad_down, losses


def gathered_shards(tokens, gate_weight, up_weight, down_frozen, down_learn, steer, sample_lengths):
    rows_tp = tokens.shape[0]
    cols = tokens.shape[1]
    width_ff = gate_weight.shape[1]
    n_tensor = lax.axis_size("tensor")
    total_rows = rows_tp * n_tensor
    seq_count = sample_lengths.shape[1]
    flat = sample_lengths.reshape(-1)
    gathered = lax.all_gather(tokens, "tensor", axis=0, tiled=True)
    every_slot = jnp.arange(total_rows, dtype=jnp.int32)
    every_len = slot_lengths(every_slot // SLOT, flat, 2 * seq_count)
    dead_key = jnp.where(every_slot % SLOT < every_len, 0, 1).astype(jnp.int32)
    live_total = 2 * (seq_count * SLOT * 5 // 8)
    source_ids = jnp.argsort(dead_key, stable=True)[:live_total]
    work_rows = jnp.take(gathered, source_ids, axis=0)
    count_rows = work_rows.shape[0]
    both_in = jnp.concatenate([gate_weight, up_weight], axis=1)
    block = work_rows
    summed = lax.psum_scatter(
        jnp.dot(block, both_in, preferred_element_type=jnp.float32),
        "fsdp",
        scatter_dimension=0,
        tiled=True,
    )
    hidden_own = (jax.nn.silu(summed[:, :width_ff]) * summed[:, width_ff:]).astype(jnp.bfloat16)
    hidden_all = lax.all_gather(hidden_own, "fsdp", axis=0, tiled=True)
    both_out = jnp.concatenate([down_frozen, down_learn], axis=1)
    own_count = count_rows // n_tensor
    block = hidden_all
    mlp_terms = lax.psum_scatter(
        jnp.dot(block, both_out, preferred_element_type=jnp.float32),
        "tensor",
        scatter_dimension=0,
        tiled=True,
    )
    own_start = lax.axis_index("tensor") * own_count
    base = lax.dynamic_slice_in_dim(work_rows, own_start, own_count, 0).astype(jnp.float32)
    out_frozen = base + mlp_terms[:, :cols]
    out_learn = base + mlp_terms[:, cols:]
    row_ids = lax.dynamic_slice_in_dim(source_ids, own_start, own_count, 0)
    row_len = slot_lengths(row_ids // SLOT, flat, 2 * seq_count)
    live = row_ids % SLOT < row_len
    forget = (live & (row_ids < seq_count * SLOT))[:, None]
    retain = (live & (row_ids >= seq_count * SLOT))[:, None]
    scale = 20.0 / jnp.sqrt(D * (jnp.mean(steer * steer) + 1e-06))
    target = scale * lax.dynamic_slice_in_dim(steer, lax.axis_index("fsdp") * cols, cols)
    steer_diff = out_learn - target[None, :]
    keep_diff = out_learn - out_frozen
    zero = jnp.zeros((), jnp.float32)
    local_steer = jnp.sum(jnp.where(forget, steer_diff * steer_diff, zero))
    local_keep = jnp.sum(jnp.where(retain, keep_diff * keep_diff, zero))
    sum_steer, sum_keep = lax.psum((local_steer, local_keep), ("fsdp", "tensor"))
    count_f = jnp.sum(sample_lengths[0]).astype(jnp.float32)
    count_r = jnp.sum(sample_lengths[1]).astype(jnp.float32)
    losses = jnp.stack([sum_steer / (count_f * D), sum_keep / (count_r * D)])
    delta = (jnp.where(forget, steer_diff, zero) + 2.0 * jnp.where(retain, keep_diff, zero)).astype(
        jnp.bfloat16
    )
    delta_all = lax.all_gather(delta, "tensor", axis=0, tiled=True)
    grad_down = lax.dot_general(
        hidden_all, delta_all, (((0,), (0,)), ((), ())), preferred_element_type=jnp.float32
    )
    return (grad_down, losses)


def solution(mesh):
    paired = mesh.shape["fsdp"] == 8 and mesh.shape["tensor"] == 4
    return jax.shard_map(
        paired_shards if paired else gathered_shards,
        mesh=mesh,
        in_specs=(
            P("tensor", "fsdp"),
            P("fsdp", "tensor"),
            P("fsdp", "tensor"),
            P("tensor", "fsdp"),
            P("tensor", "fsdp"),
            P(),
            P(),
        ),
        out_specs=(P("tensor", "fsdp"), P()),
        check_vma=False,
    )
```

```python
import math

import jax
import jax.numpy as jnp
from jax import lax
from jax.experimental import pallas as pl
from jax.experimental.pallas import tpu as pltpu
from jax.sharding import PartitionSpec as P

D = 8192
SLOT = 128
TOKEN_BOUND = 6.0
WEIGHT_BOUND = 0.0625
HALF_MAX = 65504.0
VMEM_BYTES = 8 * 1024 * 1024
IN_VMEM_BYTES = 50 * 1024 * 1024
f32 = jnp.float32
bf16 = jnp.bfloat16
f16 = jnp.float16
FIRST = (2, 4)
SECOND = (4, 2)


def slot_lengths(slot_ids, flat, sample_count):
    sample_ids = jnp.arange(sample_count, dtype=jnp.int32)
    return jnp.sum(jnp.where(slot_ids[:, None] == sample_ids[None, :], flat[None, :], 0), axis=1)


def dot(a, b):
    return jnp.dot(a, b, preferred_element_type=f32)


def swap(axis, bit, x):
    return lax.ppermute(x, axis, [(i, i ^ bit) for i in range(lax.axis_size(axis))])


def by_core(axis_bits, x):
    even, odd = axis_bits
    n = lax.axis_size("fsdp")
    return lax.ppermute(x, "fsdp", [(i, i ^ (odd if i % 2 else even)) for i in range(n)])


def after(x, *others):
    return lax.optimization_barrier((x,) + others)[0]


def in_kernel(core_ref, x1_ref, x2_ref, s1_ref, s2_ref, wg_ref, wu_ref, sg_ref, su_ref, out_ref, *, scale):
    x = jnp.concatenate([x1_ref[...], x2_ref[...]], axis=0)
    xs = jnp.concatenate([s1_ref[...], s2_ref[...]], axis=0)
    out_ref[0] = (dot(x, wg_ref[...]) + dot(xs, sg_ref[...])) * scale
    out_ref[1] = (dot(x, wu_ref[...]) + dot(xs, su_ref[...])) * scale


def in_products(core, first, first_at, second, second_at, weights, quarter, scale):
    gate_weight, up_weight, gate_sib, up_sib = weights
    cols, half = gate_sib.shape
    steps = 2
    tile = half // steps
    rows1 = pl.BlockSpec((quarter, cols), lambda j, c: (first_at(c[0]), 0))
    rows2 = pl.BlockSpec((quarter, cols), lambda j, c: (second_at(c[0]), 0))
    own = pl.BlockSpec((cols, tile), lambda j, c: (0, c[0] * steps + j))
    sib = pl.BlockSpec((cols, tile), lambda j, c: (0, j))
    return pl.pallas_call(
        lambda *refs: in_kernel(*refs, scale=scale),
        grid_spec=pltpu.PrefetchScalarGridSpec(
            num_scalar_prefetch=1,
            grid=(steps,),
            in_specs=[rows1, rows2, rows1, rows2, own, own, sib, sib],
            out_specs=pl.BlockSpec((2, 2 * quarter, tile), lambda j, c: (0, 0, j)),
        ),
        out_shape=jax.ShapeDtypeStruct((2, 2 * quarter, half), f32),
        compiler_params=pltpu.CompilerParams(vmem_limit_bytes=IN_VMEM_BYTES),
        name="in_products",
    )(core, first[0], second[0], first[1], second[1], gate_weight, up_weight, gate_sib, up_sib)


def turn_kernel(*refs):
    *parts, out_ref = refs
    out_ref[...] = jnp.concatenate([p[...] for p in parts], axis=0).T


def turned(parts):
    width = parts[0].shape[1]
    rows = sum(p.shape[0] for p in parts)
    tile = 512
    return pl.pallas_call(
        turn_kernel,
        grid=(width // tile,),
        in_specs=[pl.BlockSpec((p.shape[0], tile), lambda j: (0, j)) for p in parts],
        out_specs=pl.BlockSpec((tile, rows), lambda j: (j, 0)),
        out_shape=jax.ShapeDtypeStruct((width, rows), bf16),
        compiler_params=pltpu.CompilerParams(vmem_limit_bytes=VMEM_BYTES),
        name="turned",
    )(*parts)


def paired_shards(tokens, gate_weight, up_weight, down_frozen, down_learn, steer, sample_lengths):
    cols = tokens.shape[1]
    slots = tokens.shape[0]
    half = gate_weight.shape[1] // 2
    seqs = sample_lengths.shape[1]
    rows = seqs * SLOT * 5 // 8
    own_rows, quarter = rows // 2, rows // 4
    total = cols * lax.axis_size("fsdp")
    scale = 2.0 ** math.floor(math.log2(HALF_MAX / (TOKEN_BOUND * WEIGHT_BOUND * total)))
    me_f = lax.axis_index("fsdp")
    me_t = lax.axis_index("tensor")
    core = me_f % 2
    chip = me_f // 2
    forget_first = me_t // 2 == 0
    low_half = (me_t % 2) == (me_t // 2)
    even = core == 0
    core_arg = core.reshape(1).astype(jnp.int32)

    other_tokens = swap("tensor", 1, tokens)

    def given(w):
        return lax.dynamic_slice_in_dim(w, (1 - core) * half, half, 1)

    gate_give = given(gate_weight)
    gate_sib = swap("fsdp", 1, gate_give)
    up_give = given(after(up_weight, gate_give))
    up_sib = swap("fsdp", 1, up_give)
    weights = (gate_weight, up_weight, gate_sib, up_sib)

    lengths = jnp.where(forget_first, sample_lengths[0], sample_lengths[1])
    before = jnp.cumsum(lengths) - lengths

    def pick(block_of_slots):
        slot_ids = block_of_slots * slots + jnp.arange(slots, dtype=jnp.int32)
        sample = slot_ids // SLOT
        inside = slot_ids % SLOT
        position = slot_lengths(sample, before, seqs) + inside
        position = jnp.where(inside < slot_lengths(sample, lengths, seqs), position, -1)
        row = jnp.arange(rows, dtype=jnp.int32)
        wanted = jnp.bitwise_xor(chip, row // quarter) * quarter + row % quarter
        return (wanted[:, None] == position[None, :]).astype(bf16)

    mine = me_t % 2
    mine_rows = dot(pick(mine), after(tokens, up_give))
    other_tokens = after(other_tokens, up_give, mine_rows)
    x_a = (mine_rows + dot(pick(1 - mine), other_tokens)).astype(bf16)
    hi_a, lo_a = x_a[quarter:], x_a[:quarter]
    hi_b = swap("tensor", 3, hi_a)
    lo_b = swap("tensor", 3, lo_a)
    frozen_a = jnp.where(forget_first, 0.0, 1.0)
    frozen_b = 1.0 - frozen_a
    latest = []

    def go(*xs):
        out = lax.optimization_barrier(xs + tuple(latest))[: len(xs)]
        return out[0] if len(xs) == 1 else out

    def did(x):
        latest[:] = [x]
        return x

    class Chunk:
        def __init__(self, hi, lo):
            self.hi, self.lo = hi, lo

        def exchange_hi(self):
            self.hi = go(self.hi)
            self.hi_sib = swap("fsdp", 1, self.hi)

        def exchange_lo(self):
            self.lo = go(self.lo)
            self.lo_sib = swap("fsdp", 1, self.lo)

        def give(self):
            hi = go(self.hi, self.hi_sib)
            products = in_products(
                core_arg, hi, lambda c: c, hi, lambda c: 2, weights, quarter, scale
            )
            self.got = by_core(FIRST, did(products.astype(f16)))

        def keep(self):
            hi, lo = go(self.hi, self.hi_sib), (self.lo, self.lo_sib)
            self.kept = did(
                in_products(core_arg, lo, lambda c: 0, hi, lambda c: 1 - c, weights, quarter, scale)
            )

        def second(self):
            got, kept = go(self.got, self.kept)
            give = did((kept[:, quarter:] + got[:, quarter:].astype(f32)).astype(f16))
            self.kept = kept[:, :quarter] + got[:, :quarter].astype(f32)
            self.got = by_core(SECOND, give)

        def hidden(self):
            got, kept = go(self.got, self.kept)
            summed = (kept + got.astype(f32)) * (1.0 / scale)
            self.own = did((jax.nn.silu(summed[0]) * summed[1]).astype(bf16))
            self.got = by_core(SECOND, self.own)

        def gather_half(self):
            own, got = go(self.own, self.got)
            self.own = did(jnp.concatenate([own, got], axis=0))
            self.got = by_core(FIRST, self.own)
            self.own_sib = swap("fsdp", 1, self.own)

        def gather_whole(self):
            self.got = did(go(self.got))
            self.got_sib = swap("fsdp", 1, self.got)

        def down(self, frozen_part):
            own, got, own_sib, got_sib = go(self.own, self.got, self.own_sib, self.got_sib)

            def rows_of(want):
                def pick_rows(o, g, is_even):
                    low = jnp.concatenate([o[:quarter], jnp.where(is_even, g[:quarter], o[quarter:])], axis=0)
                    high = jnp.concatenate([jnp.where(is_even, o[quarter:], g[:quarter]), g[quarter:]], axis=0)
                    return jnp.where(want, low, high)

                mine = pick_rows(own, got, even)
                theirs = pick_rows(own_sib, got_sib, jnp.logical_not(even))
                return jnp.concatenate(
                    [jnp.where(even, mine, theirs), jnp.where(even, theirs, mine)], axis=1
                )

            def mlp(rows_in):
                return dot(rows_in, down_learn) - frozen_part * dot(rows_in, down_frozen)

            other_rows = rows_of(jnp.logical_not(low_half))
            own_rows_in = rows_of(low_half)
            give = did(mlp(other_rows).astype(bf16))
            self.got = swap("tensor", 1, give)
            self.mlp = did(mlp(go(own_rows_in)))
            self.parts = [own_rows_in, other_rows]

        def pair(self):
            mlp, got = go(self.mlp, self.got)
            give = did((mlp + got.astype(f32)).astype(bf16))
            self.far = swap("tensor", 3, give)

        def delta(self, far):
            mlp, got, far = go(self.mlp, self.got, far)
            mlp = mlp + got.astype(f32) + far.astype(f32)
            x = jnp.concatenate([self.lo, self.hi], axis=0)
            base = jnp.where(low_half, x[:own_rows], x[own_rows:]).astype(f32)
            diff = jnp.where(forget_first, mlp, base + mlp - target[None, :])
            self.loss = jnp.sum(diff * diff)
            mine = did((diff * jnp.where(forget_first, 2.0, 1.0)).astype(bf16))
            self.back = swap("tensor", 3, mine)
            self.delta_b = [mine, swap("tensor", 1, mine)]

        def turn_back(self):
            back = go(self.back)
            self.delta_a = [back, swap("tensor", 1, back)]

    mean_square = jnp.mean(steer * steer)
    target_scale = 20.0 / jnp.sqrt(total * (mean_square + 1e-06))
    target = target_scale * lax.dynamic_slice_in_dim(steer, me_f * cols, cols)

    a, b = Chunk(hi_a, lo_a), Chunk(hi_b, lo_b)
    a.exchange_hi()
    a.exchange_lo()
    a.give()
    b.exchange_hi()
    a.keep()
    a.second()
    b.give()
    b.exchange_lo()
    a.hidden()
    a.gather_half()
    b.keep()
    a.gather_whole()
    b.second()
    a.down(frozen_a)
    b.hidden()
    b.gather_half()
    a.pair()
    b.gather_whole()
    b.down(frozen_b)
    b.delta(a.far)
    value = jnp.full((8, 128), b.loss, f32)
    value = did(value + go(swap("fsdp", 2, value)))
    b.turn_back()
    value = did(value + go(swap("fsdp", 4, value)))
    value = did(value + go(swap("fsdp", 1, value)))
    value = did(value + go(swap("tensor", 1, value)))
    other = swap("tensor", 3, value)
    hidden = did(turned(list(go(*a.parts, *b.parts))))
    delta = jnp.concatenate(b.delta_a + b.delta_b, axis=0)
    grad_down = did(dot(go(hidden), delta))
    other = go(other)
    sum_steer = jnp.where(forget_first, other, value)[0, 0]
    sum_keep = jnp.where(forget_first, value, other)[0, 0]
    count_f = jnp.sum(sample_lengths[0]).astype(f32)
    count_r = jnp.sum(sample_lengths[1]).astype(f32)
    losses = jnp.stack([sum_steer / (count_f * total), sum_keep / (count_r * total)])
    return grad_down, losses


def gathered_shards(tokens, gate_weight, up_weight, down_frozen, down_learn, steer, sample_lengths):
    rows_tp = tokens.shape[0]
    cols = tokens.shape[1]
    width_ff = gate_weight.shape[1]
    n_tensor = lax.axis_size("tensor")
    total_rows = rows_tp * n_tensor
    seq_count = sample_lengths.shape[1]
    flat = sample_lengths.reshape(-1)
    gathered = lax.all_gather(tokens, "tensor", axis=0, tiled=True)
    every_slot = jnp.arange(total_rows, dtype=jnp.int32)
    every_len = slot_lengths(every_slot // SLOT, flat, 2 * seq_count)
    dead_key = jnp.where(every_slot % SLOT < every_len, 0, 1).astype(jnp.int32)
    live_total = 2 * (seq_count * SLOT * 5 // 8)
    source_ids = jnp.argsort(dead_key, stable=True)[:live_total]
    work_rows = jnp.take(gathered, source_ids, axis=0)
    count_rows = work_rows.shape[0]
    both_in = jnp.concatenate([gate_weight, up_weight], axis=1)
    block = work_rows
    summed = lax.psum_scatter(
        jnp.dot(block, both_in, preferred_element_type=jnp.float32),
        "fsdp",
        scatter_dimension=0,
        tiled=True,
    )
    hidden_own = (jax.nn.silu(summed[:, :width_ff]) * summed[:, width_ff:]).astype(jnp.bfloat16)
    hidden_all = lax.all_gather(hidden_own, "fsdp", axis=0, tiled=True)
    both_out = jnp.concatenate([down_frozen, down_learn], axis=1)
    own_count = count_rows // n_tensor
    block = hidden_all
    mlp_terms = lax.psum_scatter(
        jnp.dot(block, both_out, preferred_element_type=jnp.float32),
        "tensor",
        scatter_dimension=0,
        tiled=True,
    )
    own_start = lax.axis_index("tensor") * own_count
    base = lax.dynamic_slice_in_dim(work_rows, own_start, own_count, 0).astype(jnp.float32)
    out_frozen = base + mlp_terms[:, :cols]
    out_learn = base + mlp_terms[:, cols:]
    row_ids = lax.dynamic_slice_in_dim(source_ids, own_start, own_count, 0)
    row_len = slot_lengths(row_ids // SLOT, flat, 2 * seq_count)
    live = row_ids % SLOT < row_len
    forget = (live & (row_ids < seq_count * SLOT))[:, None]
    retain = (live & (row_ids >= seq_count * SLOT))[:, None]
    scale = 20.0 / jnp.sqrt(D * (jnp.mean(steer * steer) + 1e-06))
    target = scale * lax.dynamic_slice_in_dim(steer, lax.axis_index("fsdp") * cols, cols)
    steer_diff = out_learn - target[None, :]
    keep_diff = out_learn - out_frozen
    zero = jnp.zeros((), jnp.float32)
    local_steer = jnp.sum(jnp.where(forget, steer_diff * steer_diff, zero))
    local_keep = jnp.sum(jnp.where(retain, keep_diff * keep_diff, zero))
    sum_steer, sum_keep = lax.psum((local_steer, local_keep), ("fsdp", "tensor"))
    count_f = jnp.sum(sample_lengths[0]).astype(jnp.float32)
    count_r = jnp.sum(sample_lengths[1]).astype(jnp.float32)
    losses = jnp.stack([sum_steer / (count_f * D), sum_keep / (count_r * D)])
    delta = (jnp.where(forget, steer_diff, zero) + 2.0 * jnp.where(retain, keep_diff, zero)).astype(
        jnp.bfloat16
    )
    delta_all = lax.all_gather(delta, "tensor", axis=0, tiled=True)
    grad_down = lax.dot_general(
        hidden_all, delta_all, (((0,), (0,)), ((), ())), preferred_element_type=jnp.float32
    )
    return (grad_down, losses)


def solution(mesh):
    paired = mesh.shape["fsdp"] == 8 and mesh.shape["tensor"] == 4
    return jax.shard_map(
        paired_shards if paired else gathered_shards,
        mesh=mesh,
        in_specs=(
            P("tensor", "fsdp"),
            P("fsdp", "tensor"),
            P("fsdp", "tensor"),
            P("tensor", "fsdp"),
            P("tensor", "fsdp"),
            P(),
            P(),
        ),
        out_specs=(P("tensor", "fsdp"), P()),
        check_vma=False,
    )
```

```python
import math

import jax
import jax.numpy as jnp
from jax import lax
from jax.experimental import pallas as pl
from jax.experimental.pallas import tpu as pltpu
from jax.sharding import PartitionSpec as P

D = 8192
SLOT = 128
TOKEN_BOUND = 6.0
WEIGHT_BOUND = 0.0625
HALF_MAX = 65504.0
SIB_PARTS = 2
GRAD_VMEM_BYTES = 56 * 1024 * 1024
IN_VMEM_BYTES = 50 * 1024 * 1024
f32 = jnp.float32
bf16 = jnp.bfloat16
f16 = jnp.float16
FREE = pl.CostEstimate(flops=0, bytes_accessed=0, transcendentals=0)
FIRST = (2, 4)
SECOND = (4, 2)


def slot_lengths(slot_ids, flat, sample_count):
    sample_ids = jnp.arange(sample_count, dtype=jnp.int32)
    return jnp.sum(jnp.where(slot_ids[:, None] == sample_ids[None, :], flat[None, :], 0), axis=1)


def dot(a, b):
    return jnp.dot(a, b, preferred_element_type=f32)


def swap(axis, bit, x):
    return lax.ppermute(x, axis, [(i, i ^ bit) for i in range(lax.axis_size(axis))])


def by_core(axis_bits, x):
    even, odd = axis_bits
    n = lax.axis_size("fsdp")
    return lax.ppermute(x, "fsdp", [(i, i ^ (odd if i % 2 else even)) for i in range(n)])


def after(x, *others):
    return lax.optimization_barrier((x,) + others)[0]


def in_kernel(core_ref, x1_ref, x2_ref, s1_ref, s2_ref, wg_ref, wu_ref, *refs, scale):
    x = jnp.concatenate([x1_ref[...], x2_ref[...]], axis=0)
    xs = jnp.concatenate([s1_ref[...], s2_ref[...]], axis=0)
    *sibs, out_ref = refs
    n = len(sibs) // 2
    depth = x.shape[1] // n
    for i, own_ref in enumerate((wg_ref, wu_ref)):
        total = dot(x, own_ref[...])
        for k, sib_ref in enumerate(sibs[i * n : (i + 1) * n]):
            total += dot(xs[:, k * depth : (k + 1) * depth], sib_ref[...])
        out_ref[i] = total * scale


def in_products(core, x, x_sib, first_at, second_at, weights, quarter, scale, cost):
    gate_weight, up_weight, gate_sib, up_sib = weights
    cols = x.shape[1]
    depth, half = gate_sib[0].shape
    steps = 2
    tile = half // steps
    rows1 = pl.BlockSpec((quarter, cols), lambda j, c: (first_at(c[0]), 0))
    rows2 = pl.BlockSpec((quarter, cols), lambda j, c: (second_at(c[0]), 0))
    own = pl.BlockSpec((cols, tile), lambda j, c: (0, c[0] * steps + j))
    sib = pl.BlockSpec((depth, tile), lambda j, c: (0, j))
    return pl.pallas_call(
        lambda *refs: in_kernel(*refs, scale=scale),
        grid_spec=pltpu.PrefetchScalarGridSpec(
            num_scalar_prefetch=1,
            grid=(steps,),
            in_specs=[rows1, rows2, rows1, rows2, own, own] + [sib] * (2 * len(gate_sib)),
            out_specs=pl.BlockSpec((2, 2 * quarter, tile), lambda j, c: (0, 0, j)),
        ),
        out_shape=jax.ShapeDtypeStruct((2, 2 * quarter, half), f32),
        compiler_params=pltpu.CompilerParams(vmem_limit_bytes=IN_VMEM_BYTES),
        cost_estimate=cost,
        name="in_products",
    )(core, x, x, x_sib, x_sib, gate_weight, up_weight, *gate_sib, *up_sib)


def grad_kernel(*refs):
    *operands, out_ref = refs
    n = len(operands) // 2
    hidden = jnp.concatenate([h[...] for h in operands[:n]], axis=0)
    delta = jnp.concatenate([d[...] for d in operands[n:]], axis=0)
    out_ref[...] = lax.dot_general(
        hidden, delta, (((0,), (0,)), ((), ())), preferred_element_type=f32
    )


def grad_products(hiddens, deltas):
    width, cols = hiddens[0].shape[1], deltas[0].shape[1]
    steps = 4
    tile = width // steps
    specs = [pl.BlockSpec((h.shape[0], tile), lambda j: (0, j)) for h in hiddens]
    specs += [pl.BlockSpec(d.shape, lambda j: (0, 0)) for d in deltas]
    return pl.pallas_call(
        grad_kernel,
        grid=(steps,),
        in_specs=specs,
        out_specs=pl.BlockSpec((tile, cols), lambda j: (j, 0)),
        out_shape=jax.ShapeDtypeStruct((width, cols), f32),
        compiler_params=pltpu.CompilerParams(vmem_limit_bytes=GRAD_VMEM_BYTES),
        cost_estimate=FREE,
        name="grad_products",
    )(*hiddens, *deltas)


def paired_shards(tokens, gate_weight, up_weight, down_frozen, down_learn, steer, sample_lengths):
    cols = tokens.shape[1]
    slots = tokens.shape[0]
    half = gate_weight.shape[1] // 2
    seqs = sample_lengths.shape[1]
    rows = seqs * SLOT * 5 // 8
    own_rows, quarter = rows // 2, rows // 4
    total = cols * lax.axis_size("fsdp")
    scale = 2.0 ** math.floor(math.log2(HALF_MAX / (TOKEN_BOUND * WEIGHT_BOUND * total)))
    me_f = lax.axis_index("fsdp")
    me_t = lax.axis_index("tensor")
    core = me_f % 2
    chip = me_f // 2
    forget_first = me_t // 2 == 0
    low_half = (me_t % 2) == (me_t // 2)
    even = core == 0
    core_arg = core.reshape(1).astype(jnp.int32)

    other_tokens = swap("tensor", 1, tokens)

    def traded(w, sent):
        depth = cols // SIB_PARTS
        parts = []
        for k in range(SIB_PARTS):
            at = (k * depth, (1 - core) * half)
            sent.append(lax.dynamic_slice(after(w, *sent[-1:]), at, (depth, half)))
            parts.append(swap("fsdp", 1, sent[-1]))
        return parts

    sent = []
    gate_sib = traded(gate_weight, sent)
    up_sib = traded(up_weight, sent)
    weights = (gate_weight, up_weight, gate_sib, up_sib)

    lengths = jnp.where(forget_first, sample_lengths[0], sample_lengths[1])
    before = jnp.cumsum(lengths) - lengths

    def pick(block_of_slots):
        slot_ids = block_of_slots * slots + jnp.arange(slots, dtype=jnp.int32)
        sample = slot_ids // SLOT
        inside = slot_ids % SLOT
        position = slot_lengths(sample, before, seqs) + inside
        position = jnp.where(inside < slot_lengths(sample, lengths, seqs), position, -1)
        row = jnp.arange(rows, dtype=jnp.int32)
        wanted = jnp.bitwise_xor(chip, row // quarter) * quarter + row % quarter
        return (wanted[:, None] == position[None, :]).astype(bf16)

    mine = me_t % 2
    mine_rows = dot(pick(mine), after(tokens, sent[-1]))
    other_tokens = after(other_tokens, mine_rows)
    x_a = (mine_rows + dot(pick(1 - mine), other_tokens)).astype(bf16)
    x_b = swap("tensor", 3, x_a)
    frozen_a = jnp.where(forget_first, 0.0, 1.0)
    frozen_b = 1.0 - frozen_a
    latest = []

    def go(*xs):
        out = lax.optimization_barrier(xs + tuple(latest))[: len(xs)]
        return out[0] if len(xs) == 1 else out

    def did(x):
        latest[:] = [x]
        return x

    class Chunk:
        def __init__(self, x):
            self.x = x

        def exchange(self):
            self.x = did(go(self.x))
            self.x_sib = swap("fsdp", 1, self.x)

        def products(self, cost):
            x, x_sib = go(self.x, self.x_sib)
            self.give = did(
                in_products(core_arg, x, x_sib, lambda c: 1 + c, lambda c: 3, weights, quarter, scale, cost)
            )

        def send(self, apart):
            give = go(self.give)
            if apart:
                gives = [give[0].astype(f16), give[1].astype(f16)]
                did(gives[1])
                self.got = [by_core(FIRST, g) for g in gives]
            else:
                got = by_core(FIRST, did(give.astype(f16)))
                self.got = [got[0], got[1]]

        def keep(self, cost):
            x, x_sib = go(self.x, self.x_sib)
            self.kept = did(
                in_products(core_arg, x, x_sib, lambda c: 0, lambda c: 2 - c, weights, quarter, scale, cost)
            )

        def second(self):
            got0, got1, kept = go(*self.got, self.kept)
            sums = [kept[0] + got0.astype(f32), kept[1] + got1.astype(f32)]
            give = did(jnp.concatenate([s[quarter:] for s in sums], axis=0).astype(f16))
            self.kept = [s[:quarter] for s in sums]
            self.got = by_core(SECOND, give)

        def hidden(self):
            got, gate, up = go(self.got, *self.kept)
            gate = (gate + got[:quarter].astype(f32)) * (1.0 / scale)
            up = (up + got[quarter:].astype(f32)) * (1.0 / scale)
            self.own = did((jax.nn.silu(gate) * up).astype(bf16))
            self.got = by_core(SECOND, self.own)

        def gather_half(self):
            own, got = go(self.own, self.got)
            self.own = did(jnp.concatenate([own, got], axis=0))
            self.got = by_core(FIRST, self.own)
            self.own_sib = swap("fsdp", 1, self.own)

        def gather_whole(self):
            self.got = did(go(self.got))
            self.got_sib = swap("fsdp", 1, self.got)

        def down(self, frozen_part):
            own, got, own_sib, got_sib = go(self.own, self.got, self.own_sib, self.got_sib)

            def rows_of(want):
                def pick_rows(o, g, is_even):
                    low = jnp.concatenate([o[:quarter], jnp.where(is_even, g[:quarter], o[quarter:])], axis=0)
                    high = jnp.concatenate([jnp.where(is_even, o[quarter:], g[:quarter]), g[quarter:]], axis=0)
                    return jnp.where(want, low, high)

                mine = pick_rows(own, got, even)
                theirs = pick_rows(own_sib, got_sib, jnp.logical_not(even))
                return jnp.concatenate(
                    [jnp.where(even, mine, theirs), jnp.where(even, theirs, mine)], axis=1
                )

            def mlp(rows_in):
                return dot(rows_in, down_learn) - frozen_part * dot(rows_in, down_frozen)

            other_rows = rows_of(jnp.logical_not(low_half))
            own_rows_in = rows_of(low_half)
            give = did(mlp(other_rows).astype(bf16))
            self.got = swap("tensor", 1, give)
            self.parts = [own_rows_in, other_rows]
            self.rest = mlp

        def down_rest(self):
            self.mlp = did(self.rest(go(self.parts[0])))


        def pair(self):
            mlp, got = go(self.mlp, self.got)
            give = did((mlp + got.astype(f32)).astype(bf16))
            self.far = swap("tensor", 3, give)

        def delta(self, far):
            mlp, got, far = go(self.mlp, self.got, far)
            mlp = mlp + got.astype(f32) + far.astype(f32)
            base = jnp.where(low_half, self.x[:own_rows], self.x[own_rows:]).astype(f32)
            diff = jnp.where(forget_first, mlp, base + mlp - target[None, :])
            self.loss = jnp.sum(diff * diff)
            mine = did((diff * jnp.where(forget_first, 2.0, 1.0)).astype(bf16))
            self.back = swap("tensor", 3, mine)
            self.delta_b = [mine, swap("tensor", 1, mine)]

        def turn_back(self):
            self.delta_b[1] = did(go(self.delta_b[1]))
            back = did(go(self.back))
            self.delta_a = [back, swap("tensor", 1, back)]

    mean_square = jnp.mean(steer * steer)
    target_scale = 20.0 / jnp.sqrt(total * (mean_square + 1e-06))
    target = target_scale * lax.dynamic_slice_in_dim(steer, me_f * cols, cols)

    a, b = Chunk(x_a), Chunk(x_b)
    a.exchange()
    a.products(FREE)
    a.send(True)
    a.keep(FREE)
    b.exchange()
    a.second()
    b.products(FREE)
    a.hidden()
    b.send(False)
    a.gather_half()
    b.keep(FREE)
    a.gather_whole()
    b.second()
    a.down(frozen_a)
    b.hidden()
    a.down_rest()
    b.gather_half()
    a.pair()
    b.gather_whole()
    b.down(frozen_b)
    b.down_rest()
    b.delta(a.far)
    value = jnp.full((8, 128), b.loss, f32)
    value = did(value + go(swap("fsdp", 2, value)))
    hiddens = go(*a.parts, *b.parts)
    did(hiddens[0])
    b.turn_back()
    for bit in (4, 1):
        value = did(value + go(swap("fsdp", bit, value)))
    b.delta_a[1] = did(go(b.delta_a[1]))
    others = [swap("tensor", bit, value) for bit in (1, 2, 3)]
    grad_down = did(grad_products(hiddens, go(*b.delta_a, *b.delta_b)))
    value, *others = go(value, *others)
    same, other = (value + others[0])[0, :2], (others[1] + others[2])[0, :2]
    steer_place = jnp.arange(2, dtype=jnp.int32) == 0
    counts = jnp.sum(sample_lengths, axis=1).astype(f32) * total
    losses = jnp.where(steer_place == forget_first, other, same) / counts
    return grad_down, losses


def gathered_shards(tokens, gate_weight, up_weight, down_frozen, down_learn, steer, sample_lengths):
    rows_tp = tokens.shape[0]
    cols = tokens.shape[1]
    width_ff = gate_weight.shape[1]
    n_tensor = lax.axis_size("tensor")
    total_rows = rows_tp * n_tensor
    seq_count = sample_lengths.shape[1]
    flat = sample_lengths.reshape(-1)
    gathered = lax.all_gather(tokens, "tensor", axis=0, tiled=True)
    every_slot = jnp.arange(total_rows, dtype=jnp.int32)
    every_len = slot_lengths(every_slot // SLOT, flat, 2 * seq_count)
    dead_key = jnp.where(every_slot % SLOT < every_len, 0, 1).astype(jnp.int32)
    live_total = 2 * (seq_count * SLOT * 5 // 8)
    source_ids = jnp.argsort(dead_key, stable=True)[:live_total]
    work_rows = jnp.take(gathered, source_ids, axis=0)
    count_rows = work_rows.shape[0]
    both_in = jnp.concatenate([gate_weight, up_weight], axis=1)
    block = work_rows
    summed = lax.psum_scatter(
        jnp.dot(block, both_in, preferred_element_type=jnp.float32),
        "fsdp",
        scatter_dimension=0,
        tiled=True,
    )
    hidden_own = (jax.nn.silu(summed[:, :width_ff]) * summed[:, width_ff:]).astype(jnp.bfloat16)
    hidden_all = lax.all_gather(hidden_own, "fsdp", axis=0, tiled=True)
    both_out = jnp.concatenate([down_frozen, down_learn], axis=1)
    own_count = count_rows // n_tensor
    block = hidden_all
    mlp_terms = lax.psum_scatter(
        jnp.dot(block, both_out, preferred_element_type=jnp.float32),
        "tensor",
        scatter_dimension=0,
        tiled=True,
    )
    own_start = lax.axis_index("tensor") * own_count
    base = lax.dynamic_slice_in_dim(work_rows, own_start, own_count, 0).astype(jnp.float32)
    out_frozen = base + mlp_terms[:, :cols]
    out_learn = base + mlp_terms[:, cols:]
    row_ids = lax.dynamic_slice_in_dim(source_ids, own_start, own_count, 0)
    row_len = slot_lengths(row_ids // SLOT, flat, 2 * seq_count)
    live = row_ids % SLOT < row_len
    forget = (live & (row_ids < seq_count * SLOT))[:, None]
    retain = (live & (row_ids >= seq_count * SLOT))[:, None]
    scale = 20.0 / jnp.sqrt(D * (jnp.mean(steer * steer) + 1e-06))
    target = scale * lax.dynamic_slice_in_dim(steer, lax.axis_index("fsdp") * cols, cols)
    steer_diff = out_learn - target[None, :]
    keep_diff = out_learn - out_frozen
    zero = jnp.zeros((), jnp.float32)
    local_steer = jnp.sum(jnp.where(forget, steer_diff * steer_diff, zero))
    local_keep = jnp.sum(jnp.where(retain, keep_diff * keep_diff, zero))
    sum_steer, sum_keep = lax.psum((local_steer, local_keep), ("fsdp", "tensor"))
    count_f = jnp.sum(sample_lengths[0]).astype(jnp.float32)
    count_r = jnp.sum(sample_lengths[1]).astype(jnp.float32)
    losses = jnp.stack([sum_steer / (count_f * D), sum_keep / (count_r * D)])
    delta = (jnp.where(forget, steer_diff, zero) + 2.0 * jnp.where(retain, keep_diff, zero)).astype(
        jnp.bfloat16
    )
    delta_all = lax.all_gather(delta, "tensor", axis=0, tiled=True)
    grad_down = lax.dot_general(
        hidden_all, delta_all, (((0,), (0,)), ((), ())), preferred_element_type=jnp.float32
    )
    return (grad_down, losses)


def solution(mesh):
    paired = mesh.shape["fsdp"] == 8 and mesh.shape["tensor"] == 4
    return jax.shard_map(
        paired_shards if paired else gathered_shards,
        mesh=mesh,
        in_specs=(
            P("tensor", "fsdp"),
            P("fsdp", "tensor"),
            P("fsdp", "tensor"),
            P("tensor", "fsdp"),
            P("tensor", "fsdp"),
            P(),
            P(),
        ),
        out_specs=(P("tensor", "fsdp"), P()),
        check_vma=False,
    )
```

```python
import math

import jax
import jax.numpy as jnp
from jax import lax
from jax.experimental import pallas as pl
from jax.experimental.pallas import tpu as pltpu
from jax.sharding import PartitionSpec as P

D = 8192
SLOT = 128
TOKEN_BOUND = 6.0
WEIGHT_BOUND = 0.0625
HALF_MAX = 65504.0
SIB_PARTS = 2
GRAD_VMEM_BYTES = 56 * 1024 * 1024
IN_VMEM_BYTES = 40 * 1024 * 1024
f32 = jnp.float32
bf16 = jnp.bfloat16
f16 = jnp.float16
FREE = pl.CostEstimate(flops=0, bytes_accessed=0, transcendentals=0)
FIRST = (2, 4)
SECOND = (4, 2)


def slot_lengths(slot_ids, flat, sample_count):
    sample_ids = jnp.arange(sample_count, dtype=jnp.int32)
    return jnp.sum(jnp.where(slot_ids[:, None] == sample_ids[None, :], flat[None, :], 0), axis=1)


def dot(a, b):
    return jnp.dot(a, b, preferred_element_type=f32)


def swap(axis, bit, x):
    return lax.ppermute(x, axis, [(i, i ^ bit) for i in range(lax.axis_size(axis))])


def by_core(axis_bits, x):
    even, odd = axis_bits
    n = lax.axis_size("fsdp")
    return lax.ppermute(x, "fsdp", [(i, i ^ (odd if i % 2 else even)) for i in range(n)])


def after(x, *others):
    return lax.optimization_barrier((x,) + others)[0]


def in_kernel(core_ref, x1_ref, x2_ref, s1_ref, s2_ref, wg_ref, wu_ref, *refs, scale):
    x = jnp.concatenate([x1_ref[...], x2_ref[...]], axis=0)
    xs = jnp.concatenate([s1_ref[...], s2_ref[...]], axis=0)
    *sibs, out_ref = refs
    n = len(sibs) // 2
    depth = x.shape[1] // n
    for i, own_ref in enumerate((wg_ref, wu_ref)):
        total = dot(x, own_ref[...])
        for k, sib_ref in enumerate(sibs[i * n : (i + 1) * n]):
            total += dot(xs[:, k * depth : (k + 1) * depth], sib_ref[...])
        out_ref[i] = total * scale


def in_products(core, x, x_sib, first_at, second_at, weights, quarter, scale, cost):
    gate_weight, up_weight, gate_sib, up_sib = weights
    cols = x.shape[1]
    depth, half = gate_sib[0].shape
    steps = 2
    tile = half // steps
    rows1 = pl.BlockSpec((quarter, cols), lambda j, c: (first_at(c[0]), 0))
    rows2 = pl.BlockSpec((quarter, cols), lambda j, c: (second_at(c[0]), 0))
    own = pl.BlockSpec((cols, tile), lambda j, c: (0, c[0] * steps + j))
    sib = pl.BlockSpec((depth, tile), lambda j, c: (0, j))
    return pl.pallas_call(
        lambda *refs: in_kernel(*refs, scale=scale),
        grid_spec=pltpu.PrefetchScalarGridSpec(
            num_scalar_prefetch=1,
            grid=(steps,),
            in_specs=[rows1, rows2, rows1, rows2, own, own] + [sib] * (2 * len(gate_sib)),
            out_specs=pl.BlockSpec((2, 2 * quarter, tile), lambda j, c: (0, 0, j)),
        ),
        out_shape=jax.ShapeDtypeStruct((2, 2 * quarter, half), f32),
        compiler_params=pltpu.CompilerParams(vmem_limit_bytes=IN_VMEM_BYTES),
        cost_estimate=cost,
        name="in_products",
    )(core, x, x, x_sib, x_sib, gate_weight, up_weight, *gate_sib, *up_sib)


def grad_kernel(*refs):
    *operands, out_ref = refs
    n = len(operands) // 2
    hidden = jnp.concatenate([h[...] for h in operands[:n]], axis=0)
    delta = jnp.concatenate([d[...] for d in operands[n:]], axis=0)
    out_ref[...] = lax.dot_general(
        hidden, delta, (((0,), (0,)), ((), ())), preferred_element_type=f32
    )


def grad_products(hiddens, deltas):
    width, cols = hiddens[0].shape[1], deltas[0].shape[1]
    steps = 4
    tile = width // steps
    specs = [pl.BlockSpec((h.shape[0], tile), lambda j: (0, j)) for h in hiddens]
    specs += [pl.BlockSpec(d.shape, lambda j: (0, 0)) for d in deltas]
    return pl.pallas_call(
        grad_kernel,
        grid=(steps,),
        in_specs=specs,
        out_specs=pl.BlockSpec((tile, cols), lambda j: (j, 0)),
        out_shape=jax.ShapeDtypeStruct((width, cols), f32),
        compiler_params=pltpu.CompilerParams(vmem_limit_bytes=GRAD_VMEM_BYTES),
        cost_estimate=FREE,
        name="grad_products",
    )(*hiddens, *deltas)


def paired_shards(tokens, gate_weight, up_weight, down_frozen, down_learn, steer, sample_lengths):
    cols = tokens.shape[1]
    slots = tokens.shape[0]
    half = gate_weight.shape[1] // 2
    seqs = sample_lengths.shape[1]
    rows = seqs * SLOT * 5 // 8
    own_rows, quarter = rows // 2, rows // 4
    total = cols * lax.axis_size("fsdp")
    scale = 2.0 ** math.floor(math.log2(HALF_MAX / (TOKEN_BOUND * WEIGHT_BOUND * total)))
    me_f = lax.axis_index("fsdp")
    me_t = lax.axis_index("tensor")
    core = me_f % 2
    chip = me_f // 2
    forget_first = me_t // 2 == 0
    low_half = (me_t % 2) == (me_t // 2)
    even = core == 0
    core_arg = core.reshape(1).astype(jnp.int32)

    other_tokens = swap("tensor", 1, tokens)

    def traded(w, sent):
        depth = cols // SIB_PARTS
        parts = []
        for k in range(SIB_PARTS):
            at = (k * depth, (1 - core) * half)
            sent.append(lax.dynamic_slice(after(w, *sent[-1:]), at, (depth, half)))
            parts.append(swap("fsdp", 1, sent[-1]))
        return parts

    sent = []
    gate_sib = traded(gate_weight, sent)
    up_sib = traded(up_weight, sent)
    weights = (gate_weight, up_weight, gate_sib, up_sib)

    lengths = jnp.where(forget_first, sample_lengths[0], sample_lengths[1])
    before = jnp.cumsum(lengths) - lengths

    def pick(block_of_slots):
        slot_ids = block_of_slots * slots + jnp.arange(slots, dtype=jnp.int32)
        sample = slot_ids // SLOT
        inside = slot_ids % SLOT
        position = slot_lengths(sample, before, seqs) + inside
        position = jnp.where(inside < slot_lengths(sample, lengths, seqs), position, -1)
        row = jnp.arange(rows, dtype=jnp.int32)
        wanted = jnp.bitwise_xor(chip, row // quarter) * quarter + row % quarter
        return (wanted[:, None] == position[None, :]).astype(bf16)

    mine = me_t % 2
    mine_rows = dot(pick(mine), after(tokens, sent[-1]))
    other_tokens = after(other_tokens, mine_rows)
    x_a = (mine_rows + dot(pick(1 - mine), other_tokens)).astype(bf16)
    x_b = swap("tensor", 3, x_a)
    frozen_a = jnp.where(forget_first, 0.0, 1.0)
    frozen_b = 1.0 - frozen_a
    latest = []

    def go(*xs):
        out = lax.optimization_barrier(xs + tuple(latest))[: len(xs)]
        return out[0] if len(xs) == 1 else out

    def did(x):
        latest[:] = [x]
        return x

    class Chunk:
        def __init__(self, x):
            self.x = x

        def exchange(self):
            self.x = did(go(self.x))
            self.x_sib = swap("fsdp", 1, self.x)

        def products(self, cost):
            x, x_sib = go(self.x, self.x_sib)
            self.give = did(
                in_products(core_arg, x, x_sib, lambda c: 1 + c, lambda c: 3, weights, quarter, scale, cost)
            )

        def send(self, apart):
            give = go(self.give)
            if apart:
                gives = [give[0].astype(f16), give[1].astype(f16)]
                did(gives[1])
                self.got = [by_core(FIRST, g) for g in gives]
            else:
                got = by_core(FIRST, did(give.astype(f16)))
                self.got = [got[0], got[1]]

        def keep(self, cost):
            x, x_sib = go(self.x, self.x_sib)
            self.kept = did(
                in_products(core_arg, x, x_sib, lambda c: 0, lambda c: 2 - c, weights, quarter, scale, cost)
            )

        def second(self):
            got0, got1, kept = go(*self.got, self.kept)
            sums = [kept[0] + got0.astype(f32), kept[1] + got1.astype(f32)]
            give = did(jnp.concatenate([s[quarter:] for s in sums], axis=0).astype(f16))
            self.kept = [s[:quarter] for s in sums]
            self.got = by_core(SECOND, give)

        def hidden(self):
            got, gate, up = go(self.got, *self.kept)
            gate = (gate + got[:quarter].astype(f32)) * (1.0 / scale)
            up = (up + got[quarter:].astype(f32)) * (1.0 / scale)
            self.own = did((jax.nn.silu(gate) * up).astype(bf16))
            self.got = by_core(SECOND, self.own)

        def gather_half(self):
            own, got = go(self.own, self.got)
            self.own = did(jnp.concatenate([own, got], axis=0))
            self.got = by_core(FIRST, self.own)
            self.own_sib = swap("fsdp", 1, self.own)

        def gather_whole(self):
            self.got = did(go(self.got))
            self.got_sib = swap("fsdp", 1, self.got)

        def down(self, frozen_part):
            own, got, own_sib, got_sib = go(self.own, self.got, self.own_sib, self.got_sib)

            def rows_of(want):
                def pick_rows(o, g, is_even):
                    low = jnp.concatenate([o[:quarter], jnp.where(is_even, g[:quarter], o[quarter:])], axis=0)
                    high = jnp.concatenate([jnp.where(is_even, o[quarter:], g[:quarter]), g[quarter:]], axis=0)
                    return jnp.where(want, low, high)

                mine = pick_rows(own, got, even)
                theirs = pick_rows(own_sib, got_sib, jnp.logical_not(even))
                return jnp.concatenate(
                    [jnp.where(even, mine, theirs), jnp.where(even, theirs, mine)], axis=1
                )

            def mlp(rows_in):
                return dot(rows_in, down_learn) - frozen_part * dot(rows_in, down_frozen)

            other_rows = rows_of(jnp.logical_not(low_half))
            own_rows_in = rows_of(low_half)
            give = did(mlp(other_rows).astype(bf16))
            self.got = swap("tensor", 1, give)
            self.parts = [own_rows_in, other_rows]
            self.rest = mlp

        def down_rest(self):
            self.mlp = did(self.rest(go(self.parts[0])))


        def pair(self):
            mlp, got = go(self.mlp, self.got)
            give = did((mlp + got.astype(f32)).astype(bf16))
            self.far = swap("tensor", 3, give)

        def delta(self, far):
            mlp, got, far = go(self.mlp, self.got, far)
            mlp = mlp + got.astype(f32) + far.astype(f32)
            base = jnp.where(low_half, self.x[:own_rows], self.x[own_rows:]).astype(f32)
            diff = jnp.where(forget_first, mlp, base + mlp - target[None, :])
            self.loss = jnp.sum(diff * diff)
            mine = did((diff * jnp.where(forget_first, 2.0, 1.0)).astype(bf16))
            self.back = swap("tensor", 3, mine)
            self.delta_b = [mine, swap("tensor", 1, mine)]

        def turn_back(self):
            back = did(go(self.back))
            self.delta_a = [back, swap("tensor", 1, back)]
            self.delta_b[1] = did(go(self.delta_b[1]))

    mean_square = jnp.mean(steer * steer)
    target_scale = 20.0 / jnp.sqrt(total * (mean_square + 1e-06))
    target = target_scale * lax.dynamic_slice_in_dim(steer, me_f * cols, cols)

    a, b = Chunk(x_a), Chunk(x_b)
    a.exchange()
    a.products(FREE)
    a.send(True)
    a.keep(FREE)
    b.exchange()
    a.second()
    b.products(FREE)
    a.hidden()
    b.send(False)
    a.gather_half()
    b.keep(FREE)
    a.gather_whole()
    b.second()
    a.down(frozen_a)
    b.hidden()
    a.down_rest()
    b.gather_half()
    a.pair()
    b.gather_whole()
    b.down(frozen_b)
    b.down_rest()
    b.delta(a.far)
    value = jnp.full((8, 128), b.loss, f32)
    value = did(value + go(swap("fsdp", 2, value)))
    hiddens = go(*a.parts, *b.parts)
    did(hiddens[0])
    b.turn_back()
    for bit in (4, 1):
        value = did(value + go(swap("fsdp", bit, value)))
    b.delta_a[1] = did(go(b.delta_a[1]))
    others = [swap("tensor", bit, value) for bit in (1, 2, 3)]
    grad_down = did(grad_products(hiddens, go(*b.delta_a, *b.delta_b)))
    value, *others = go(value, *others)
    same, other = (value + others[0])[0, :2], (others[1] + others[2])[0, :2]
    steer_place = jnp.arange(2, dtype=jnp.int32) == 0
    counts = jnp.sum(sample_lengths, axis=1).astype(f32) * total
    losses = jnp.where(steer_place == forget_first, other, same) / counts
    return grad_down, losses


def gathered_shards(tokens, gate_weight, up_weight, down_frozen, down_learn, steer, sample_lengths):
    rows_tp = tokens.shape[0]
    cols = tokens.shape[1]
    width_ff = gate_weight.shape[1]
    n_tensor = lax.axis_size("tensor")
    total_rows = rows_tp * n_tensor
    seq_count = sample_lengths.shape[1]
    flat = sample_lengths.reshape(-1)
    gathered = lax.all_gather(tokens, "tensor", axis=0, tiled=True)
    every_slot = jnp.arange(total_rows, dtype=jnp.int32)
    every_len = slot_lengths(every_slot // SLOT, flat, 2 * seq_count)
    dead_key = jnp.where(every_slot % SLOT < every_len, 0, 1).astype(jnp.int32)
    live_total = 2 * (seq_count * SLOT * 5 // 8)
    source_ids = jnp.argsort(dead_key, stable=True)[:live_total]
    work_rows = jnp.take(gathered, source_ids, axis=0)
    count_rows = work_rows.shape[0]
    both_in = jnp.concatenate([gate_weight, up_weight], axis=1)
    block = work_rows
    summed = lax.psum_scatter(
        jnp.dot(block, both_in, preferred_element_type=jnp.float32),
        "fsdp",
        scatter_dimension=0,
        tiled=True,
    )
    hidden_own = (jax.nn.silu(summed[:, :width_ff]) * summed[:, width_ff:]).astype(jnp.bfloat16)
    hidden_all = lax.all_gather(hidden_own, "fsdp", axis=0, tiled=True)
    both_out = jnp.concatenate([down_frozen, down_learn], axis=1)
    own_count = count_rows // n_tensor
    block = hidden_all
    mlp_terms = lax.psum_scatter(
        jnp.dot(block, both_out, preferred_element_type=jnp.float32),
        "tensor",
        scatter_dimension=0,
        tiled=True,
    )
    own_start = lax.axis_index("tensor") * own_count
    base = lax.dynamic_slice_in_dim(work_rows, own_start, own_count, 0).astype(jnp.float32)
    out_frozen = base + mlp_terms[:, :cols]
    out_learn = base + mlp_terms[:, cols:]
    row_ids = lax.dynamic_slice_in_dim(source_ids, own_start, own_count, 0)
    row_len = slot_lengths(row_ids // SLOT, flat, 2 * seq_count)
    live = row_ids % SLOT < row_len
    forget = (live & (row_ids < seq_count * SLOT))[:, None]
    retain = (live & (row_ids >= seq_count * SLOT))[:, None]
    scale = 20.0 / jnp.sqrt(D * (jnp.mean(steer * steer) + 1e-06))
    target = scale * lax.dynamic_slice_in_dim(steer, lax.axis_index("fsdp") * cols, cols)
    steer_diff = out_learn - target[None, :]
    keep_diff = out_learn - out_frozen
    zero = jnp.zeros((), jnp.float32)
    local_steer = jnp.sum(jnp.where(forget, steer_diff * steer_diff, zero))
    local_keep = jnp.sum(jnp.where(retain, keep_diff * keep_diff, zero))
    sum_steer, sum_keep = lax.psum((local_steer, local_keep), ("fsdp", "tensor"))
    count_f = jnp.sum(sample_lengths[0]).astype(jnp.float32)
    count_r = jnp.sum(sample_lengths[1]).astype(jnp.float32)
    losses = jnp.stack([sum_steer / (count_f * D), sum_keep / (count_r * D)])
    delta = (jnp.where(forget, steer_diff, zero) + 2.0 * jnp.where(retain, keep_diff, zero)).astype(
        jnp.bfloat16
    )
    delta_all = lax.all_gather(delta, "tensor", axis=0, tiled=True)
    grad_down = lax.dot_general(
        hidden_all, delta_all, (((0,), (0,)), ((), ())), preferred_element_type=jnp.float32
    )
    return (grad_down, losses)


def solution(mesh):
    paired = mesh.shape["fsdp"] == 8 and mesh.shape["tensor"] == 4
    return jax.shard_map(
        paired_shards if paired else gathered_shards,
        mesh=mesh,
        in_specs=(
            P("tensor", "fsdp"),
            P("fsdp", "tensor"),
            P("fsdp", "tensor"),
            P("tensor", "fsdp"),
            P("tensor", "fsdp"),
            P(),
            P(),
        ),
        out_specs=(P("tensor", "fsdp"), P()),
        check_vma=False,
    )
```

```python
import math

import jax
import jax.numpy as jnp
from jax import lax
from jax.experimental import pallas as pl
from jax.experimental.pallas import tpu as pltpu
from jax.sharding import PartitionSpec as P

D = 8192
SLOT = 128
TOKEN_BOUND = 6.0
WEIGHT_BOUND = 0.0625
HALF_MAX = 65504.0
SIB_PARTS = 2
GRAD_VMEM_BYTES = 56 * 1024 * 1024
IN_VMEM_BYTES = 40 * 1024 * 1024
f32 = jnp.float32
bf16 = jnp.bfloat16
f16 = jnp.float16
FREE = pl.CostEstimate(flops=0, bytes_accessed=0, transcendentals=0)
FIRST = (2, 4)
SECOND = (4, 2)


def slot_lengths(slot_ids, flat, sample_count):
    sample_ids = jnp.arange(sample_count, dtype=jnp.int32)
    return jnp.sum(jnp.where(slot_ids[:, None] == sample_ids[None, :], flat[None, :], 0), axis=1)


def dot(a, b):
    return jnp.dot(a, b, preferred_element_type=f32)


def swap(axis, bit, x):
    return lax.ppermute(x, axis, [(i, i ^ bit) for i in range(lax.axis_size(axis))])


def by_core(axis_bits, x):
    even, odd = axis_bits
    n = lax.axis_size("fsdp")
    return lax.ppermute(x, "fsdp", [(i, i ^ (odd if i % 2 else even)) for i in range(n)])


def after(x, *others):
    return lax.optimization_barrier((x,) + others)[0]


def in_kernel(core_ref, x1_ref, x2_ref, s1_ref, s2_ref, wg_ref, wu_ref, *refs, scale):
    x = jnp.concatenate([x1_ref[...], x2_ref[...]], axis=0)
    xs = jnp.concatenate([s1_ref[...], s2_ref[...]], axis=0)
    *sibs, out_ref = refs
    n = len(sibs) // 2
    depth = x.shape[1] // n
    for i, own_ref in enumerate((wg_ref, wu_ref)):
        total = dot(x, own_ref[...])
        for k, sib_ref in enumerate(sibs[i * n : (i + 1) * n]):
            total += dot(xs[:, k * depth : (k + 1) * depth], sib_ref[...])
        out_ref[i] = total * scale


def in_products(core, first, first_at, second, second_at, weights, quarter, scale, cost):
    gate_weight, up_weight, gate_sib, up_sib = weights
    cols = first[0].shape[1]
    depth, half = gate_sib[0].shape
    steps = 2
    tile = half // steps
    rows1 = pl.BlockSpec((quarter, cols), lambda j, c: (first_at(c[0]), 0))
    rows2 = pl.BlockSpec((quarter, cols), lambda j, c: (second_at(c[0]), 0))
    own = pl.BlockSpec((cols, tile), lambda j, c: (0, c[0] * steps + j))
    sib = pl.BlockSpec((depth, tile), lambda j, c: (0, j))
    return pl.pallas_call(
        lambda *refs: in_kernel(*refs, scale=scale),
        grid_spec=pltpu.PrefetchScalarGridSpec(
            num_scalar_prefetch=1,
            grid=(steps,),
            in_specs=[rows1, rows2, rows1, rows2, own, own] + [sib] * (2 * len(gate_sib)),
            out_specs=pl.BlockSpec((2, 2 * quarter, tile), lambda j, c: (0, 0, j)),
        ),
        out_shape=jax.ShapeDtypeStruct((2, 2 * quarter, half), f32),
        compiler_params=pltpu.CompilerParams(vmem_limit_bytes=IN_VMEM_BYTES),
        cost_estimate=cost,
        name="in_products",
    )(core, first[0], second[0], first[1], second[1], gate_weight, up_weight, *gate_sib, *up_sib)


def grad_kernel(*refs):
    *operands, out_ref = refs
    n = len(operands) // 2
    hidden = jnp.concatenate([h[...] for h in operands[:n]], axis=0)
    delta = jnp.concatenate([d[...] for d in operands[n:]], axis=0)
    out_ref[...] = lax.dot_general(
        hidden, delta, (((0,), (0,)), ((), ())), preferred_element_type=f32
    )


def grad_products(hiddens, deltas):
    width, cols = hiddens[0].shape[1], deltas[0].shape[1]
    steps = 4
    tile = width // steps
    specs = [pl.BlockSpec((h.shape[0], tile), lambda j: (0, j)) for h in hiddens]
    specs += [pl.BlockSpec(d.shape, lambda j: (0, 0)) for d in deltas]
    return pl.pallas_call(
        grad_kernel,
        grid=(steps,),
        in_specs=specs,
        out_specs=pl.BlockSpec((tile, cols), lambda j: (j, 0)),
        out_shape=jax.ShapeDtypeStruct((width, cols), f32),
        compiler_params=pltpu.CompilerParams(vmem_limit_bytes=GRAD_VMEM_BYTES),
        cost_estimate=FREE,
        name="grad_products",
    )(*hiddens, *deltas)


def paired_shards(tokens, gate_weight, up_weight, down_frozen, down_learn, steer, sample_lengths):
    cols = tokens.shape[1]
    slots = tokens.shape[0]
    half = gate_weight.shape[1] // 2
    seqs = sample_lengths.shape[1]
    rows = seqs * SLOT * 5 // 8
    own_rows, quarter = rows // 2, rows // 4
    total = cols * lax.axis_size("fsdp")
    scale = 2.0 ** math.floor(math.log2(HALF_MAX / (TOKEN_BOUND * WEIGHT_BOUND * total)))
    me_f = lax.axis_index("fsdp")
    me_t = lax.axis_index("tensor")
    core = me_f % 2
    chip = me_f // 2
    forget_first = me_t // 2 == 0
    low_half = (me_t % 2) == (me_t // 2)
    even = core == 0
    core_arg = core.reshape(1).astype(jnp.int32)

    other_tokens = swap("tensor", 1, tokens)

    def traded(w, sent):
        depth = cols // SIB_PARTS
        parts = []
        for k in range(SIB_PARTS):
            at = (k * depth, (1 - core) * half)
            sent.append(lax.dynamic_slice(after(w, *sent[-1:]), at, (depth, half)))
            parts.append(swap("fsdp", 1, sent[-1]))
        return parts

    sent = []
    gate_sib = traded(gate_weight, sent)
    up_sib = traded(up_weight, sent)
    weights = (gate_weight, up_weight, gate_sib, up_sib)

    lengths = jnp.where(forget_first, sample_lengths[0], sample_lengths[1])
    before = jnp.cumsum(lengths) - lengths

    def pick(block_of_slots):
        slot_ids = block_of_slots * slots + jnp.arange(slots, dtype=jnp.int32)
        sample = slot_ids // SLOT
        inside = slot_ids % SLOT
        position = slot_lengths(sample, before, seqs) + inside
        position = jnp.where(inside < slot_lengths(sample, lengths, seqs), position, -1)
        row = jnp.arange(rows, dtype=jnp.int32)
        wanted = jnp.bitwise_xor(chip, row // quarter) * quarter + row % quarter
        return (wanted[:, None] == position[None, :]).astype(bf16)

    mine = me_t % 2
    mine_rows = dot(pick(mine), after(tokens, sent[-1]))
    other_tokens = after(other_tokens, mine_rows)
    x_a = (mine_rows + dot(pick(1 - mine), other_tokens)).astype(bf16)
    hi_b = swap("tensor", 3, x_a[quarter:])
    lo_b = swap("tensor", 3, x_a[:quarter])
    frozen_a = jnp.where(forget_first, 0.0, 1.0)
    frozen_b = 1.0 - frozen_a
    latest = []

    def go(*xs):
        out = lax.optimization_barrier(xs + tuple(latest))[: len(xs)]
        return out[0] if len(xs) == 1 else out

    def did(x):
        latest[:] = [x]
        return x

    class Chunk:
        def __init__(self, lo, hi, at):
            self.lo, self.hi, self.at = lo, hi, at

        def exchange(self):
            self.hi = did(go(self.hi))
            self.hi_sib = swap("fsdp", 1, self.hi)
            if self.lo is None:
                self.lo, self.lo_sib = self.hi, self.hi_sib

        def exchange_lo(self):
            self.lo = did(go(self.lo))
            self.lo_sib = swap("fsdp", 1, self.lo)

        def products(self, cost):
            hi, at = go(self.hi, self.hi_sib), self.at
            self.give = did(
                in_products(
                    core_arg, hi, lambda c: at + c, hi, lambda c: at + 2, weights, quarter, scale, cost
                )
            )

        def send(self, apart):
            give = go(self.give)
            if apart:
                gives = [give[k, r : r + quarter].astype(f16) for k in range(2) for r in (0, quarter)]
                did(gives[-1])
                self.got = [by_core(FIRST, g) for g in gives]
            else:
                got = by_core(FIRST, did(give.astype(f16)))
                self.got = [got[k, r : r + quarter] for k in range(2) for r in (0, quarter)]

        def keep(self, cost):
            lo, lo_sib, hi, hi_sib = go(self.lo, self.lo_sib, self.hi, self.hi_sib)
            at = self.at
            self.kept = did(
                in_products(
                    core_arg, (lo, lo_sib), lambda c: 0, (hi, hi_sib), lambda c: at + 1 - c, weights, quarter, scale, cost
                )
            )

        def second(self):
            *got, kept = go(*self.got, self.kept)
            gives = [kept[k, quarter:] + got[2 * k + 1].astype(f32) for k in range(2)]
            give = did(jnp.concatenate(gives, axis=0).astype(f16))
            self.kept = [kept[k, :quarter] + got[2 * k].astype(f32) for k in range(2)]
            self.got = by_core(SECOND, give)

        def hidden(self):
            got, gate, up = go(self.got, *self.kept)
            gate = (gate + got[:quarter].astype(f32)) * (1.0 / scale)
            up = (up + got[quarter:].astype(f32)) * (1.0 / scale)
            self.own = did((jax.nn.silu(gate) * up).astype(bf16))
            self.got = by_core(SECOND, self.own)

        def gather_half(self):
            own, got = go(self.own, self.got)
            self.own = did(jnp.concatenate([own, got], axis=0))
            self.got = by_core(FIRST, self.own)
            self.own_sib = swap("fsdp", 1, self.own)

        def gather_whole(self):
            self.got = did(go(self.got))
            self.got_sib = swap("fsdp", 1, self.got)

        def down(self, frozen_part):
            own, got, own_sib, got_sib = go(self.own, self.got, self.own_sib, self.got_sib)

            def rows_of(want):
                def pick_rows(o, g, is_even):
                    low = jnp.concatenate([o[:quarter], jnp.where(is_even, g[:quarter], o[quarter:])], axis=0)
                    high = jnp.concatenate([jnp.where(is_even, o[quarter:], g[:quarter]), g[quarter:]], axis=0)
                    return jnp.where(want, low, high)

                mine = pick_rows(own, got, even)
                theirs = pick_rows(own_sib, got_sib, jnp.logical_not(even))
                return jnp.concatenate(
                    [jnp.where(even, mine, theirs), jnp.where(even, theirs, mine)], axis=1
                )

            def mlp(rows_in):
                return dot(rows_in, down_learn) - frozen_part * dot(rows_in, down_frozen)

            other_rows = rows_of(jnp.logical_not(low_half))
            own_rows_in = rows_of(low_half)
            give = did(mlp(other_rows).astype(bf16))
            self.got = swap("tensor", 1, give)
            self.parts = [own_rows_in, other_rows]
            self.rest = mlp

        def down_rest(self):
            self.mlp = did(self.rest(go(self.parts[0])))


        def pair(self):
            mlp, got = go(self.mlp, self.got)
            give = did((mlp + got.astype(f32)).astype(bf16))
            self.far = swap("tensor", 3, give)

        def delta(self, far):
            mlp, got, far = go(self.mlp, self.got, far)
            mlp = mlp + got.astype(f32) + far.astype(f32)
            x = jnp.concatenate([self.lo, self.hi], axis=0)
            base = jnp.where(low_half, x[:own_rows], x[own_rows:]).astype(f32)
            diff = jnp.where(forget_first, mlp, base + mlp - target[None, :])
            self.loss = jnp.sum(diff * diff)
            mine = did((diff * jnp.where(forget_first, 2.0, 1.0)).astype(bf16))
            self.back = swap("tensor", 3, mine)
            self.delta_b = [mine, swap("tensor", 1, mine)]

        def turn_back(self):
            back = did(go(self.back))
            self.delta_a = [back, swap("tensor", 1, back)]
            self.delta_b[1] = did(go(self.delta_b[1]))

    mean_square = jnp.mean(steer * steer)
    target_scale = 20.0 / jnp.sqrt(total * (mean_square + 1e-06))
    target = target_scale * lax.dynamic_slice_in_dim(steer, me_f * cols, cols)

    a, b = Chunk(None, x_a, 1), Chunk(lo_b, hi_b, 0)
    a.exchange()
    a.products(FREE)
    a.send(True)
    a.keep(FREE)
    b.exchange()
    a.second()
    b.products(FREE)
    a.hidden()
    b.send(False)
    b.exchange_lo()
    a.gather_half()
    b.keep(FREE)
    a.gather_whole()
    b.second()
    a.down(frozen_a)
    b.hidden()
    a.down_rest()
    b.gather_half()
    a.pair()
    b.gather_whole()
    b.down(frozen_b)
    b.down_rest()
    b.delta(a.far)
    value = jnp.full((8, 128), b.loss, f32)
    value = did(value + go(swap("fsdp", 2, value)))
    hiddens = go(*a.parts, *b.parts)
    did(hiddens[0])
    b.turn_back()
    for bit in (4, 1):
        value = did(value + go(swap("fsdp", bit, value)))
    b.delta_a[1] = did(go(b.delta_a[1]))
    others = [swap("tensor", bit, value) for bit in (1, 2, 3)]
    grad_down = did(grad_products(hiddens, go(*b.delta_a, *b.delta_b)))
    value, *others = go(value, *others)
    same, other = (value + others[0])[0, :2], (others[1] + others[2])[0, :2]
    steer_place = jnp.arange(2, dtype=jnp.int32) == 0
    counts = jnp.sum(sample_lengths, axis=1).astype(f32) * total
    losses = jnp.where(steer_place == forget_first, other, same) / counts
    return grad_down, losses


def gathered_shards(tokens, gate_weight, up_weight, down_frozen, down_learn, steer, sample_lengths):
    rows_tp = tokens.shape[0]
    cols = tokens.shape[1]
    width_ff = gate_weight.shape[1]
    n_tensor = lax.axis_size("tensor")
    total_rows = rows_tp * n_tensor
    seq_count = sample_lengths.shape[1]
    flat = sample_lengths.reshape(-1)
    gathered = lax.all_gather(tokens, "tensor", axis=0, tiled=True)
    every_slot = jnp.arange(total_rows, dtype=jnp.int32)
    every_len = slot_lengths(every_slot // SLOT, flat, 2 * seq_count)
    dead_key = jnp.where(every_slot % SLOT < every_len, 0, 1).astype(jnp.int32)
    live_total = 2 * (seq_count * SLOT * 5 // 8)
    source_ids = jnp.argsort(dead_key, stable=True)[:live_total]
    work_rows = jnp.take(gathered, source_ids, axis=0)
    count_rows = work_rows.shape[0]
    both_in = jnp.concatenate([gate_weight, up_weight], axis=1)
    block = work_rows
    summed = lax.psum_scatter(
        jnp.dot(block, both_in, preferred_element_type=jnp.float32),
        "fsdp",
        scatter_dimension=0,
        tiled=True,
    )
    hidden_own = (jax.nn.silu(summed[:, :width_ff]) * summed[:, width_ff:]).astype(jnp.bfloat16)
    hidden_all = lax.all_gather(hidden_own, "fsdp", axis=0, tiled=True)
    both_out = jnp.concatenate([down_frozen, down_learn], axis=1)
    own_count = count_rows // n_tensor
    block = hidden_all
    mlp_terms = lax.psum_scatter(
        jnp.dot(block, both_out, preferred_element_type=jnp.float32),
        "tensor",
        scatter_dimension=0,
        tiled=True,
    )
    own_start = lax.axis_index("tensor") * own_count
    base = lax.dynamic_slice_in_dim(work_rows, own_start, own_count, 0).astype(jnp.float32)
    out_frozen = base + mlp_terms[:, :cols]
    out_learn = base + mlp_terms[:, cols:]
    row_ids = lax.dynamic_slice_in_dim(source_ids, own_start, own_count, 0)
    row_len = slot_lengths(row_ids // SLOT, flat, 2 * seq_count)
    live = row_ids % SLOT < row_len
    forget = (live & (row_ids < seq_count * SLOT))[:, None]
    retain = (live & (row_ids >= seq_count * SLOT))[:, None]
    scale = 20.0 / jnp.sqrt(D * (jnp.mean(steer * steer) + 1e-06))
    target = scale * lax.dynamic_slice_in_dim(steer, lax.axis_index("fsdp") * cols, cols)
    steer_diff = out_learn - target[None, :]
    keep_diff = out_learn - out_frozen
    zero = jnp.zeros((), jnp.float32)
    local_steer = jnp.sum(jnp.where(forget, steer_diff * steer_diff, zero))
    local_keep = jnp.sum(jnp.where(retain, keep_diff * keep_diff, zero))
    sum_steer, sum_keep = lax.psum((local_steer, local_keep), ("fsdp", "tensor"))
    count_f = jnp.sum(sample_lengths[0]).astype(jnp.float32)
    count_r = jnp.sum(sample_lengths[1]).astype(jnp.float32)
    losses = jnp.stack([sum_steer / (count_f * D), sum_keep / (count_r * D)])
    delta = (jnp.where(forget, steer_diff, zero) + 2.0 * jnp.where(retain, keep_diff, zero)).astype(
        jnp.bfloat16
    )
    delta_all = lax.all_gather(delta, "tensor", axis=0, tiled=True)
    grad_down = lax.dot_general(
        hidden_all, delta_all, (((0,), (0,)), ((), ())), preferred_element_type=jnp.float32
    )
    return (grad_down, losses)


def solution(mesh):
    paired = mesh.shape["fsdp"] == 8 and mesh.shape["tensor"] == 4
    return jax.shard_map(
        paired_shards if paired else gathered_shards,
        mesh=mesh,
        in_specs=(
            P("tensor", "fsdp"),
            P("fsdp", "tensor"),
            P("fsdp", "tensor"),
            P("tensor", "fsdp"),
            P("tensor", "fsdp"),
            P(),
            P(),
        ),
        out_specs=(P("tensor", "fsdp"), P()),
        check_vma=False,
    )
```

```python
import math

import jax
import jax.numpy as jnp
from jax import lax
from jax.experimental import pallas as pl
from jax.experimental.pallas import tpu as pltpu
from jax.sharding import PartitionSpec as P

D = 8192
SLOT = 128
TOKEN_BOUND = 6.0
WEIGHT_BOUND = 0.0625
HALF_MAX = 65504.0
SIB_PARTS = 2
GRAD_VMEM_BYTES = 56 * 1024 * 1024
IN_VMEM_BYTES = 40 * 1024 * 1024
f32 = jnp.float32
bf16 = jnp.bfloat16
f16 = jnp.float16
FREE = pl.CostEstimate(flops=0, bytes_accessed=0, transcendentals=0)
FIRST = (2, 4)
SECOND = (4, 2)


def slot_lengths(slot_ids, flat, sample_count):
    sample_ids = jnp.arange(sample_count, dtype=jnp.int32)
    return jnp.sum(jnp.where(slot_ids[:, None] == sample_ids[None, :], flat[None, :], 0), axis=1)


def dot(a, b):
    return jnp.dot(a, b, preferred_element_type=f32)


def swap(axis, bit, x):
    return lax.ppermute(x, axis, [(i, i ^ bit) for i in range(lax.axis_size(axis))])


def by_core(axis_bits, x):
    even, odd = axis_bits
    n = lax.axis_size("fsdp")
    return lax.ppermute(x, "fsdp", [(i, i ^ (odd if i % 2 else even)) for i in range(n)])


def after(x, *others):
    return lax.optimization_barrier((x,) + others)[0]


def in_kernel(core_ref, x1_ref, x2_ref, s1_ref, s2_ref, wg_ref, wu_ref, *refs, scale):
    x = jnp.concatenate([x1_ref[...], x2_ref[...]], axis=0)
    xs = jnp.concatenate([s1_ref[...], s2_ref[...]], axis=0)
    *sibs, out_ref = refs
    n = len(sibs) // 2
    depth = x.shape[1] // n
    for i, own_ref in enumerate((wg_ref, wu_ref)):
        total = dot(x, own_ref[...])
        for k, sib_ref in enumerate(sibs[i * n : (i + 1) * n]):
            total += dot(xs[:, k * depth : (k + 1) * depth], sib_ref[...])
        out_ref[i] = total * scale


def in_products(core, first, first_at, second, second_at, weights, quarter, scale, cost):
    gate_weight, up_weight, gate_sib, up_sib = weights
    cols = first[0].shape[1]
    depth, half = gate_sib[0].shape
    steps = 2
    tile = half // steps
    rows1 = pl.BlockSpec((quarter, cols), lambda j, c: (first_at(c[0]), 0))
    rows2 = pl.BlockSpec((quarter, cols), lambda j, c: (second_at(c[0]), 0))
    own = pl.BlockSpec((cols, tile), lambda j, c: (0, c[0] * steps + j))
    sib = pl.BlockSpec((depth, tile), lambda j, c: (0, j))
    return pl.pallas_call(
        lambda *refs: in_kernel(*refs, scale=scale),
        grid_spec=pltpu.PrefetchScalarGridSpec(
            num_scalar_prefetch=1,
            grid=(steps,),
            in_specs=[rows1, rows2, rows1, rows2, own, own] + [sib] * (2 * len(gate_sib)),
            out_specs=pl.BlockSpec((2, 2 * quarter, tile), lambda j, c: (0, 0, j)),
        ),
        out_shape=jax.ShapeDtypeStruct((2, 2 * quarter, half), f32),
        compiler_params=pltpu.CompilerParams(vmem_limit_bytes=IN_VMEM_BYTES),
        cost_estimate=cost,
        name="in_products",
    )(core, first[0], second[0], first[1], second[1], gate_weight, up_weight, *gate_sib, *up_sib)


def grad_kernel(*refs):
    *operands, out_ref = refs
    n = len(operands) // 2
    hidden = jnp.concatenate([h[...] for h in operands[:n]], axis=0)
    delta = jnp.concatenate([d[...] for d in operands[n:]], axis=0)
    out_ref[...] = lax.dot_general(
        hidden, delta, (((0,), (0,)), ((), ())), preferred_element_type=f32
    )


def grad_products(hiddens, deltas):
    width, cols = hiddens[0].shape[1], deltas[0].shape[1]
    steps = 4
    tile = width // steps
    specs = [pl.BlockSpec((h.shape[0], tile), lambda j: (0, j)) for h in hiddens]
    specs += [pl.BlockSpec(d.shape, lambda j: (0, 0)) for d in deltas]
    return pl.pallas_call(
        grad_kernel,
        grid=(steps,),
        in_specs=specs,
        out_specs=pl.BlockSpec((tile, cols), lambda j: (j, 0)),
        out_shape=jax.ShapeDtypeStruct((width, cols), f32),
        compiler_params=pltpu.CompilerParams(vmem_limit_bytes=GRAD_VMEM_BYTES),
        name="grad_products",
    )(*hiddens, *deltas)


def paired_shards(tokens, gate_weight, up_weight, down_frozen, down_learn, steer, sample_lengths):
    cols = tokens.shape[1]
    slots = tokens.shape[0]
    half = gate_weight.shape[1] // 2
    seqs = sample_lengths.shape[1]
    rows = seqs * SLOT * 5 // 8
    own_rows, quarter = rows // 2, rows // 4
    total = cols * lax.axis_size("fsdp")
    scale = 2.0 ** math.floor(math.log2(HALF_MAX / (TOKEN_BOUND * WEIGHT_BOUND * total)))
    me_f = lax.axis_index("fsdp")
    me_t = lax.axis_index("tensor")
    core = me_f % 2
    chip = me_f // 2
    forget_first = me_t // 2 == 0
    low_half = (me_t % 2) == (me_t // 2)
    even = core == 0
    core_arg = core.reshape(1).astype(jnp.int32)

    other_tokens = swap("tensor", 1, tokens)

    def traded(w, sent):
        depth = cols // SIB_PARTS
        parts = []
        for k in range(SIB_PARTS):
            at = (k * depth, (1 - core) * half)
            sent.append(lax.dynamic_slice(after(w, *sent[-1:]), at, (depth, half)))
            parts.append(swap("fsdp", 1, sent[-1]))
        return parts

    sent = []
    gate_sib = traded(gate_weight, sent)
    up_sib = traded(up_weight, sent)
    weights = (gate_weight, up_weight, gate_sib, up_sib)

    lengths = jnp.where(forget_first, sample_lengths[0], sample_lengths[1])
    before = jnp.cumsum(lengths) - lengths

    def pick(block_of_slots):
        slot_ids = block_of_slots * slots + jnp.arange(slots, dtype=jnp.int32)
        sample = slot_ids // SLOT
        inside = slot_ids % SLOT
        position = slot_lengths(sample, before, seqs) + inside
        position = jnp.where(inside < slot_lengths(sample, lengths, seqs), position, -1)
        row = jnp.arange(rows, dtype=jnp.int32)
        wanted = jnp.bitwise_xor(chip, row // quarter) * quarter + row % quarter
        return (wanted[:, None] == position[None, :]).astype(bf16)

    mine = me_t % 2
    mine_rows = dot(pick(mine), after(tokens, sent[-1]))
    other_tokens = after(other_tokens, mine_rows)
    x_a = (mine_rows + dot(pick(1 - mine), other_tokens)).astype(bf16)
    hi_b = swap("tensor", 3, x_a[quarter:])
    lo_b = swap("tensor", 3, x_a[:quarter])
    frozen_a = jnp.where(forget_first, 0.0, 1.0)
    frozen_b = 1.0 - frozen_a
    latest = []

    def go(*xs):
        out = lax.optimization_barrier(xs + tuple(latest))[: len(xs)]
        return out[0] if len(xs) == 1 else out

    def did(x):
        latest[:] = [x]
        return x

    class Chunk:
        def __init__(self, lo, hi, at):
            self.lo, self.hi, self.at = lo, hi, at

        def exchange(self):
            self.hi = did(go(self.hi))
            self.hi_sib = swap("fsdp", 1, self.hi)
            if self.lo is None:
                self.lo, self.lo_sib = self.hi, self.hi_sib

        def exchange_lo(self):
            self.lo = did(go(self.lo))
            self.lo_sib = swap("fsdp", 1, self.lo)

        def products(self, cost):
            hi, at = go(self.hi, self.hi_sib), self.at
            self.give = did(
                in_products(
                    core_arg, hi, lambda c: at + c, hi, lambda c: at + 2, weights, quarter, scale, cost
                )
            )

        def send(self, apart):
            give = go(self.give)
            if apart:
                gives = [give[k, r : r + quarter].astype(f16) for k in range(2) for r in (0, quarter)]
                did(gives[-1])
                self.got = [by_core(FIRST, g) for g in gives]
            else:
                got = by_core(FIRST, did(give.astype(f16)))
                self.got = [got[k, r : r + quarter] for k in range(2) for r in (0, quarter)]

        def keep(self, cost):
            lo, lo_sib, hi, hi_sib = go(self.lo, self.lo_sib, self.hi, self.hi_sib)
            at = self.at
            self.kept = did(
                in_products(
                    core_arg, (lo, lo_sib), lambda c: 0, (hi, hi_sib), lambda c: at + 1 - c, weights, quarter, scale, cost
                )
            )

        def second(self):
            *got, kept = go(*self.got, self.kept)
            gives = [kept[k, quarter:] + got[2 * k + 1].astype(f32) for k in range(2)]
            give = did(jnp.concatenate(gives, axis=0).astype(f16))
            self.kept = [kept[k, :quarter] + got[2 * k].astype(f32) for k in range(2)]
            self.got = by_core(SECOND, give)

        def hidden(self):
            got, gate, up = go(self.got, *self.kept)
            gate = (gate + got[:quarter].astype(f32)) * (1.0 / scale)
            up = (up + got[quarter:].astype(f32)) * (1.0 / scale)
            self.own = did((jax.nn.silu(gate) * up).astype(bf16))
            self.got = by_core(SECOND, self.own)

        def gather_half(self):
            own, got = go(self.own, self.got)
            self.own = did(jnp.concatenate([own, got], axis=0))
            self.got = by_core(FIRST, self.own)
            self.own_sib = swap("fsdp", 1, self.own)

        def gather_whole(self):
            self.got = did(go(self.got))
            self.got_sib = swap("fsdp", 1, self.got)

        def down(self, frozen_part):
            own, got, own_sib, got_sib = go(self.own, self.got, self.own_sib, self.got_sib)

            def rows_of(want):
                def pick_rows(o, g, is_even):
                    low = jnp.concatenate([o[:quarter], jnp.where(is_even, g[:quarter], o[quarter:])], axis=0)
                    high = jnp.concatenate([jnp.where(is_even, o[quarter:], g[:quarter]), g[quarter:]], axis=0)
                    return jnp.where(want, low, high)

                mine = pick_rows(own, got, even)
                theirs = pick_rows(own_sib, got_sib, jnp.logical_not(even))
                return jnp.concatenate(
                    [jnp.where(even, mine, theirs), jnp.where(even, theirs, mine)], axis=1
                )

            def mlp(rows_in):
                return dot(rows_in, down_learn) - frozen_part * dot(rows_in, down_frozen)

            other_rows = rows_of(jnp.logical_not(low_half))
            own_rows_in = rows_of(low_half)
            give = did(mlp(other_rows).astype(bf16))
            self.got = swap("tensor", 1, give)
            self.parts = [own_rows_in, other_rows]
            self.rest = mlp

        def down_rest(self):
            self.mlp = did(self.rest(go(self.parts[0])))


        def pair(self):
            mlp, got = go(self.mlp, self.got)
            give = did((mlp + got.astype(f32)).astype(bf16))
            self.far = swap("tensor", 3, give)

        def delta(self, far):
            mlp, got, far = go(self.mlp, self.got, far)
            mlp = mlp + got.astype(f32) + far.astype(f32)
            x = jnp.concatenate([self.lo, self.hi], axis=0)
            base = jnp.where(low_half, x[:own_rows], x[own_rows:]).astype(f32)
            diff = jnp.where(forget_first, mlp, base + mlp - target[None, :])
            self.loss = jnp.sum(diff * diff)
            mine = did((diff * jnp.where(forget_first, 2.0, 1.0)).astype(bf16))
            self.back = swap("tensor", 3, mine)
            self.delta_b = [mine, swap("tensor", 1, mine)]

        def turn_back(self):
            back = did(go(self.back))
            self.delta_a = [back, swap("tensor", 1, back)]
            self.delta_b[1] = did(go(self.delta_b[1]))

    mean_square = jnp.mean(steer * steer)
    target_scale = 20.0 / jnp.sqrt(total * (mean_square + 1e-06))
    target = target_scale * lax.dynamic_slice_in_dim(steer, me_f * cols, cols)

    a, b = Chunk(None, x_a, 1), Chunk(lo_b, hi_b, 0)
    a.exchange()
    a.products(FREE)
    a.send(True)
    a.keep(FREE)
    b.exchange()
    a.second()
    b.products(FREE)
    a.hidden()
    b.send(False)
    b.exchange_lo()
    a.gather_half()
    b.keep(FREE)
    a.gather_whole()
    b.second()
    a.down(frozen_a)
    b.hidden()
    a.down_rest()
    b.gather_half()
    a.pair()
    b.gather_whole()
    b.down(frozen_b)
    b.down_rest()
    a.parts = list(go(*a.parts))
    did(a.parts[0])
    b.delta(a.far)
    value = jnp.full((8, 128), b.loss, f32)
    value = did(value + go(swap("fsdp", 2, value)))
    hiddens = go(*a.parts, *b.parts)
    did(hiddens[0])
    b.turn_back()
    for bit in (4, 1):
        value = did(value + go(swap("fsdp", bit, value)))
    b.delta_a[1] = did(go(b.delta_a[1]))
    others = [swap("tensor", bit, value) for bit in (1, 2, 3)]
    grad_down = did(grad_products(hiddens, go(*b.delta_a, *b.delta_b)))
    value, *others = go(value, *others)
    same, other = (value + others[0])[0, :2], (others[1] + others[2])[0, :2]
    steer_place = jnp.arange(2, dtype=jnp.int32) == 0
    counts = jnp.sum(sample_lengths, axis=1).astype(f32) * total
    losses = jnp.where(steer_place == forget_first, other, same) / counts
    return grad_down, losses


def gathered_shards(tokens, gate_weight, up_weight, down_frozen, down_learn, steer, sample_lengths):
    rows_tp = tokens.shape[0]
    cols = tokens.shape[1]
    width_ff = gate_weight.shape[1]
    n_tensor = lax.axis_size("tensor")
    total_rows = rows_tp * n_tensor
    seq_count = sample_lengths.shape[1]
    flat = sample_lengths.reshape(-1)
    gathered = lax.all_gather(tokens, "tensor", axis=0, tiled=True)
    every_slot = jnp.arange(total_rows, dtype=jnp.int32)
    every_len = slot_lengths(every_slot // SLOT, flat, 2 * seq_count)
    dead_key = jnp.where(every_slot % SLOT < every_len, 0, 1).astype(jnp.int32)
    live_total = 2 * (seq_count * SLOT * 5 // 8)
    source_ids = jnp.argsort(dead_key, stable=True)[:live_total]
    work_rows = jnp.take(gathered, source_ids, axis=0)
    count_rows = work_rows.shape[0]
    both_in = jnp.concatenate([gate_weight, up_weight], axis=1)
    block = work_rows
    summed = lax.psum_scatter(
        jnp.dot(block, both_in, preferred_element_type=jnp.float32),
        "fsdp",
        scatter_dimension=0,
        tiled=True,
    )
    hidden_own = (jax.nn.silu(summed[:, :width_ff]) * summed[:, width_ff:]).astype(jnp.bfloat16)
    hidden_all = lax.all_gather(hidden_own, "fsdp", axis=0, tiled=True)
    both_out = jnp.concatenate([down_frozen, down_learn], axis=1)
    own_count = count_rows // n_tensor
    block = hidden_all
    mlp_terms = lax.psum_scatter(
        jnp.dot(block, both_out, preferred_element_type=jnp.float32),
        "tensor",
        scatter_dimension=0,
        tiled=True,
    )
    own_start = lax.axis_index("tensor") * own_count
    base = lax.dynamic_slice_in_dim(work_rows, own_start, own_count, 0).astype(jnp.float32)
    out_frozen = base + mlp_terms[:, :cols]
    out_learn = base + mlp_terms[:, cols:]
    row_ids = lax.dynamic_slice_in_dim(source_ids, own_start, own_count, 0)
    row_len = slot_lengths(row_ids // SLOT, flat, 2 * seq_count)
    live = row_ids % SLOT < row_len
    forget = (live & (row_ids < seq_count * SLOT))[:, None]
    retain = (live & (row_ids >= seq_count * SLOT))[:, None]
    scale = 20.0 / jnp.sqrt(D * (jnp.mean(steer * steer) + 1e-06))
    target = scale * lax.dynamic_slice_in_dim(steer, lax.axis_index("fsdp") * cols, cols)
    steer_diff = out_learn - target[None, :]
    keep_diff = out_learn - out_frozen
    zero = jnp.zeros((), jnp.float32)
    local_steer = jnp.sum(jnp.where(forget, steer_diff * steer_diff, zero))
    local_keep = jnp.sum(jnp.where(retain, keep_diff * keep_diff, zero))
    sum_steer, sum_keep = lax.psum((local_steer, local_keep), ("fsdp", "tensor"))
    count_f = jnp.sum(sample_lengths[0]).astype(jnp.float32)
    count_r = jnp.sum(sample_lengths[1]).astype(jnp.float32)
    losses = jnp.stack([sum_steer / (count_f * D), sum_keep / (count_r * D)])
    delta = (jnp.where(forget, steer_diff, zero) + 2.0 * jnp.where(retain, keep_diff, zero)).astype(
        jnp.bfloat16
    )
    delta_all = lax.all_gather(delta, "tensor", axis=0, tiled=True)
    grad_down = lax.dot_general(
        hidden_all, delta_all, (((0,), (0,)), ((), ())), preferred_element_type=jnp.float32
    )
    return (grad_down, losses)


def solution(mesh):
    paired = mesh.shape["fsdp"] == 8 and mesh.shape["tensor"] == 4
    return jax.shard_map(
        paired_shards if paired else gathered_shards,
        mesh=mesh,
        in_specs=(
            P("tensor", "fsdp"),
            P("fsdp", "tensor"),
            P("fsdp", "tensor"),
            P("tensor", "fsdp"),
            P("tensor", "fsdp"),
            P(),
            P(),
        ),
        out_specs=(P("tensor", "fsdp"), P()),
        check_vma=False,
    )
```
